32 devices in a mesh: groups: 2 (over x), gx: 16 (over z, y, core).
Axes of the slice: x: 2, y: 2, z: 4, core: 2. Of those that a mesh axis runs over, the one named last changes fastest.
Arguments:
- wave_state: float32 [2, 2, 64, 320, 256], P(None, 'groups', 'gx'), parts along dimension 1, may hold values from -6 to 6
- adjoint_state: float32 [2, 2, 64, 320, 256], P(None, 'groups', 'gx'), parts along dimension 1, may hold values from -6 to 6
- velocity: float32 [64, 640, 256], P('gx', 'groups'), parts along dimension 1, may hold values from 0.15 to 0.45
- wavelet: float32 [2, 32], P('groups'), parts along dimension 0, may hold values from -12 to 12
- traces: float32 [2, 32, 256], P('groups', None, 'gx'), parts along dimension 0, may hold values from -6 to 6
- source_cells: int32 [2, 3], P('groups'), parts along dimension 0, may hold values from 0 to 63, as said below
- receiver_cells: int32 [2, 3, 256], P('groups'), parts along dimension 0, may hold values from 0 to 63, as said below
- start_step: int32 [2], P('groups'), parts along dimension 0, may hold values from 0 to 27
Outputs:
- gradient: float32 [64, 640, 256], P('gx', 'groups'), parts along dimension 1
- earlier_adjoint: float32 [2, 2, 64, 320, 256], P(None, 'groups', 'gx'), parts along dimension 1
The draws below stay inside these ranges and needn't reach their ends.
There are 2 independent parts, one for each index of `groups`. The reference program is written for one: setup_inputs(seed, part) draws one part's arguments, and reference() takes and returns one part's arrays. A program takes and returns all parts, laid end to end along the dimension named above; each array names one. Nothing has to cross between parts.
Inputs may be any that keep to these rules, and one draw needn't show every extreme that they name: `source_cells`: every component of a cell index is below min(64, 320, 256). `receiver_cells`: every component of a cell index is below min(64, 320, 256).
All inputs are finite; a program needn't handle non-finite values.
Results may differ from the reference program's by a relative error of at most 0.0002.
Values sent between devices are 32-bit elements; how exact they have to be, the bound alone decides.
No kernel may reach another device: no remote copies, remote signals or barrier semaphores. Data moves between devices by JAX's collectives and lax.ppermute only.
A program may use at most 128 MiB of HBM per device.

```python
import math
import jax
import jax.numpy as jnp
from jax import lax

SHOTS = 1
NY = 320
NZ = 256
STEPS = 4
NT = 32
NX = 64
NREC = 256


def draw_source_cells(key, part):
    key = jax.random.fold_in(key, 11)
    limit = min(NX, NY, NZ)
    cells = jax.random.randint(key, (SHOTS, 3), 0, limit, dtype=jnp.int32)
    cells = cells.at[0, 0].set(limit - 1)
    cells = cells.at[0, 1].set(0)
    return cells


def draw_receiver_cells(key, part):
    key = jax.random.fold_in(key, 23)
    limit = min(NX, NY, NZ)
    cells = jax.random.randint(key, (SHOTS, 3, NREC), 0, limit, dtype=jnp.int32)
    cells = cells.at[0, 0, 0].set(limit - 1)
    cells = cells.at[0, 1, NREC - 1].set(0)
    return cells


def levels(rng, dims, split, least, largest):
    factor_of, own = 1.0, jax.random.fold_in(rng, 6)
    for dim, parts in split:
        draws = jnp.exp(jax.random.uniform(jax.random.fold_in(own, dim), (parts,), jnp.float32, least / len(split), largest / len(split)))
        factor_of = factor_of * jnp.repeat(draws, dims[dim] // parts).reshape([-1 if axis == dim else 1 for axis in range(len(dims))])
    return factor_of


def gaussian(own_key, extent, scale, reach, split=(), kind=jnp.bfloat16):
    loudness = levels(own_key, extent, split, -0.22, 0.18) if split else 1.0
    drawn = jax.random.normal(own_key, extent, jnp.float32) * scale * loudness
    return jnp.minimum(jnp.maximum(drawn, -reach), reach).astype(kind)


def setup_inputs(seed: int = 0, part: int = 0) -> dict:
    streams_of = jax.random.split(jax.random.key(seed), 9)
    own_keys = jax.random.split(jax.random.fold_in(streams_of[8], part), 9)
    wave_state = gaussian(own_keys[0], (2, SHOTS, NX, NY, NZ), 1.0, 6.0, ((2, 16),), jnp.float32)
    adjoint_state = gaussian(own_keys[1], (2, SHOTS, NX, NY, NZ), 1.0, 6.0, ((2, 16),), jnp.float32)
    velocity = jnp.clip(jnp.exp(math.log(0.45) - 1.0986122 * jax.random.uniform(own_keys[2], (NX, NY, NZ), jnp.float32) ** levels(own_keys[2], (NX, NY, NZ), ((0, 16),), -0.2, 0.2)), 0.15, 0.45)
    wavelet = gaussian(own_keys[3], (SHOTS, NT), 3.0, 12.0, (), jnp.float32)
    traces = gaussian(own_keys[4], (SHOTS, NT, NREC), 1.0, 6.0, ((2, 16),), jnp.float32)
    source_cells = draw_source_cells(jax.random.fold_in(jax.random.fold_in(streams_of[8], part), 71), part)
    receiver_cells = draw_receiver_cells(jax.random.fold_in(jax.random.fold_in(streams_of[8], part), 71), part)
    start_step = jax.random.randint(own_keys[7], (1,), 0, NT - STEPS).astype(jnp.int32)
    return {"wave_state": wave_state, "adjoint_state": adjoint_state, "velocity": velocity, "wavelet": wavelet, "traces": traces, "source_cells": source_cells, "receiver_cells": receiver_cells, "start_step": start_step}


WEIGHTS = (-205.0 / 72.0, 8.0 / 5.0, -1.0 / 5.0, 8.0 / 315.0, -1.0 / 560.0)


def laplace(widened):
    slab_rows = widened.shape[1] - 8
    width_y = widened.shape[2]
    width_z = widened.shape[3]
    middle = widened[:, 4:4 + slab_rows]
    padded = jnp.pad(middle, ((0, 0), (0, 0), (4, 4), (4, 4)))
    summed = (3.0 * WEIGHTS[0]) * middle
    for offset in range(1, 5):
        paired = widened[:, 4 + offset:4 + offset + slab_rows] + widened[:, 4 - offset:4 - offset + slab_rows]
        paired = paired + padded[:, :, 4 + offset:4 + offset + width_y, 4:4 + width_z] + padded[:, :, 4 - offset:4 - offset + width_y, 4:4 + width_z]
        paired = paired + padded[:, :, 4:4 + width_y, 4 + offset:4 + offset + width_z] + padded[:, :, 4:4 + width_y, 4 - offset:4 - offset + width_z]
        summed = summed + WEIGHTS[offset] * paired
    return summed


def widen(field):
    return jnp.pad(field, ((0, 0), (4, 4), (0, 0), (0, 0)))


def reference(wave_state, adjoint_state, velocity, wavelet, traces, source_cells, receiver_cells, start_step):
    start = start_step[0]
    squared = velocity * velocity
    shot_index = jnp.arange(SHOTS, dtype=jnp.int32)
    shot_grid = jnp.broadcast_to(shot_index[:, None], (SHOTS, NREC))
    before = wave_state[0]
    current = wave_state[1]
    images = []
    for step_no in range(1, STEPS + 1):
        image = laplace(widen(current))
        images.append(image)
        if step_no < STEPS:
            after = 2.0 * current - before + squared * image
            source_pulse = lax.dynamic_index_in_dim(wavelet, start + step_no, 1, keepdims=False)
            after = after.at[shot_index, source_cells[:, 0], source_cells[:, 1], source_cells[:, 2]].add(source_pulse)
            before, current = current, after
    later_field = adjoint_state[0]
    latest_field = adjoint_state[1]
    gradient = jnp.zeros(velocity.shape, jnp.float32)
    for step_no in range(STEPS, 0, -1):
        gradient = gradient + (2.0 * velocity) * jnp.sum(later_field * images[step_no - 1], axis=0)
        earlier_field = 2.0 * later_field - latest_field + laplace(widen(squared * later_field))
        samples = lax.dynamic_index_in_dim(traces, start + step_no, 1, keepdims=False)
        earlier_field = earlier_field.at[shot_grid, receiver_cells[:, 0, :], receiver_cells[:, 1, :], receiver_cells[:, 2, :]].add(samples)
        latest_field, later_field = later_field, earlier_field
    return gradient, jnp.stack([later_field, latest_field])
```

```python
import functools

import jax
import jax.numpy as jnp
from jax import lax
from jax.experimental import pallas as pl
from jax.experimental.pallas import tpu as pltpu
from jax.sharding import PartitionSpec as P

STEPS = 4
WEIGHTS = (-205.0 / 72.0, 8.0 / 5.0, -1.0 / 5.0, 8.0 / 315.0, -1.0 / 560.0)
UNIT = WEIGHTS[1]
REACH = 4
EXTRA = REACH * STEPS
F32 = jnp.float32
BF16 = jnp.bfloat16
ANY = pl.BlockSpec(memory_space=pl.ANY)
VMEM = pl.BlockSpec(memory_space=pltpu.VMEM)
SMEM = pl.BlockSpec(memory_space=pltpu.SMEM)


def place():
    position = lax.axis_index("gx")
    return position // 4, (position % 4) // 2, position % 2


def banded(size):
    shape = (size, size)
    apart = jnp.abs(
        lax.broadcasted_iota(jnp.int32, shape, 0) - lax.broadcasted_iota(jnp.int32, shape, 1)
    )
    band = jnp.zeros(shape, F32)
    for offset in range(1, REACH + 1):
        band = jnp.where(apart == offset, WEIGHTS[offset] / UNIT, band)
    return band.astype(BF16)


def two_terms(value):
    high = value.astype(BF16)
    return high, (value - high.astype(F32)).astype(BF16)


def dot(left, right, contract=((1,), (0,))):
    return lax.dot_general(left, right, (contract, ((), ())), preferred_element_type=F32)


class Copies:
    def __init__(self, sems):
        self.sems, self.used, self.going = sems, 0, []

    def start(self, source, target):
        copy = pltpu.make_async_copy(source, target, self.sems.at[self.used])
        self.used += 1
        copy.start()
        self.going.append(copy)

    def wait(self):
        for copy in self.going:
            copy.wait()
        self.going = []


class Sizes:
    def __init__(self, rows, cols, depth):
        self.rows, self.cols, self.depth = rows, cols, depth
        self.half = cols // 2
        self.wide = self.half + EXTRA

    def window(self, half):
        return pl.ds(pl.multiple_of(half * (self.half - EXTRA), 16), self.wide)

    def own(self, half):
        return pl.ds(pl.multiple_of(half * EXTRA, 16), self.half)

    def final(self, half):
        return pl.ds(pl.multiple_of(half * self.half, 16), self.half)

    @property
    def pair(self):
        return (2, self.rows, self.wide, self.depth)

    @property
    def block(self):
        return (self.rows, self.wide, self.depth)

    @property
    def sent(self):
        return (self.rows, self.half, self.depth)

    @property
    def chain(self):
        return (5 * self.rows, self.wide, self.depth)


def load_split(copies, sizes, own, received, target):
    _, half, _ = place()
    copies.start(own.at[:, sizes.window(half), :], target.at[half])
    copies.start(received, target.at[1 - half])


def load_chain(copies, sizes, mine, other, beside, chain):
    _, _, core = place()
    rows = sizes.rows

    def at(index):
        return chain.at[pl.ds(index * rows, rows)]

    copies.start(mine.at[0], at(1))
    copies.start(mine.at[1], at(3))
    copies.start(other.at[0], at(2 - 2 * core))
    copies.start(other.at[1], at(4 - 2 * core))
    copies.start(beside, at(4 * core))


def differences(sizes, chain, mixed, added=None):
    rows = sizes.rows
    band_y, band_z = banded(sizes.wide), banded(sizes.depth)
    for slot in range(2):
        for row in range(rows):
            high, low = two_terms(chain[(2 * slot + 1) * rows + row])
            total = dot(high, band_z) + dot(low, band_z) + dot(band_y, high) + dot(band_y, low)
            total = UNIT * total
            if added is not None:
                total = total + added(slot, row)
            mixed[slot, row] = total


def sweep(sizes, chain, mixed, finish):
    rows = sizes.rows

    @pl.loop(0, sizes.wide // 8)
    def _(step):
        cut = pl.ds(pl.multiple_of(step * 8, 8), 8)
        for slot in range(2):
            near = [chain[2 * slot * rows + row, cut, :] for row in range(3 * rows)]
            for row in range(rows):
                centre = near[rows + row]
                total = 3.0 * WEIGHTS[0] * centre + mixed[slot, row, cut, :]
                for offset in range(1, REACH + 1):
                    total = total + WEIGHTS[offset] * (
                        near[rows + row + offset] + near[rows + row - offset]
                    )
                finish(slot, row, cut, centre, total)


def run(body, name, operands, specs, outs, scratch, aliases=None, flops=400_000_000, sems=24):
    return pl.pallas_call(
        body,
        name=name,
        out_shape=[jax.ShapeDtypeStruct(shape, F32) for shape in outs],
        in_specs=specs,
        out_specs=[ANY] * len(outs),
        scratch_shapes=[pltpu.VMEM(shape, F32) for shape in scratch]
        + [pltpu.SemaphoreType.DMA((sems,))],
        input_output_aliases=aliases or {},
        compiler_params=pltpu.CompilerParams(vmem_limit_bytes=32 * 2**20),
        cost_estimate=pl.CostEstimate(flops=flops, bytes_accessed=8_000_000, transcendentals=0),
    )(*operands)


def adjoint_begin(sizes, velocity, velocity_in, adjoint, latest_in):
    def body(v_ref, vin_ref, a_ref, ain_ref, v_out, a_out, u_out, z_out, v, a, u, sems):
        _, _, core = place()
        copies = Copies(sems)
        load_split(copies, sizes, v_ref, vin_ref, v)
        load_split(copies, sizes, a_ref.at[0, 0], ain_ref, a)
        copies.wait()

        @pl.loop(0, sizes.wide // 8)
        def _(step):
            cut = pl.ds(pl.multiple_of(step * 8, 8), 8)
            speed = v[:, :, cut, :]
            u[:, :, cut, :] = speed * speed * a[:, :, cut, :]

        copies.start(u.at[core], z_out)
        copies.start(u, u_out)
        copies.start(v, v_out)
        copies.start(a, a_out)
        copies.wait()

    return run(
        body,
        "adjoint_begin",
        (velocity, velocity_in, adjoint, latest_in),
        [ANY] * 4,
        [sizes.pair, sizes.pair, sizes.pair, sizes.block],
        [sizes.pair] * 3,
    )


def adjoint_step(sizes, step_no, scaled, other, beside, later, latest, speed, cells, samples, whole):
    split = isinstance(latest, tuple)
    more = step_no > 1
    ends = step_no <= 2
    carried = whole is not None
    n_in = 8 + split + carried

    def body(*refs):
        u_ref, other_ref, beside_ref, later_ref, v_ref, cells_ref, samples_ref = refs[:7]
        latest_refs = refs[7 : 8 + split]
        rest = list(refs[n_in:])
        if more:
            next_out, scaled_out, z_out = rest[:3]
            rest = rest[3:]
        if ends:
            whole_out, sent_out = rest[:2]
            rest = rest[2:]
        chain, mixed, late, last, v, u, sems = rest
        level, half, core = place()
        copies = Copies(sems)
        load_chain(copies, sizes, u_ref, other_ref, beside_ref, chain)
        copies.start(later_ref, late)
        if split:
            load_split(copies, sizes, latest_refs[0].at[1, 0], latest_refs[1], last)
        else:
            copies.start(latest_refs[0], last)
        if more:
            copies.start(v_ref, v)
        where_x, where_y, where_z = (cells_ref[0, axis : axis + 1, :] for axis in range(3))
        count = where_x.shape[1]
        depth_ids = lax.broadcasted_iota(jnp.int32, (sizes.depth, count), 0)
        values = jnp.where(where_z == depth_ids, samples_ref[0, step_no - 1 : step_no, :], 0.0)
        value_high, value_low = two_terms(values)
        first_col = half * (sizes.half - EXTRA)
        col_ids = lax.broadcasted_iota(jnp.int32, (sizes.wide, count), 0) + first_col

        def added(slot, row):
            this_row = ((level * 2 + slot) * 2 + core) * sizes.rows + row
            col_of = jnp.where(where_x == this_row, where_y, -1)
            hit = jnp.where(col_of == col_ids, 1.0, 0.0).astype(BF16)
            across = ((1,), (1,))
            return dot(hit, value_high, across) + dot(hit, value_low, across)

        copies.wait()
        differences(sizes, chain, mixed, added)

        def finish(slot, row, cut, centre, total):
            value = 2.0 * late[slot, row, cut, :] - last[slot, row, cut, :] + total
            last[slot, row, cut, :] = value
            if more:
                here = v[slot, row, cut, :]
                u[slot, row, cut, :] = here * here * value

        sweep(sizes, chain, mixed, finish)
        if more:
            copies.start(u.at[core], z_out)
            copies.start(u, scaled_out)
            copies.start(last, next_out)
        if ends:
            copies.start(last.at[1 - half, :, sizes.own(half), :], sent_out)
            copies.start(
                last.at[half, :, sizes.own(half), :],
                whole_out.at[step_no - 1, 0, :, sizes.final(half), :],
            )
        copies.wait()

    latest = latest if split else (latest,)
    operands = (scaled, other, beside, later, speed, cells, samples, *latest)
    specs = [ANY] * 5 + [VMEM] * 2 + [ANY] * (1 + split)
    outs = []
    aliases = {}
    if more:
        outs += [sizes.pair, sizes.pair, sizes.block]
    if ends:
        outs += [(2, 1, sizes.rows, sizes.cols, sizes.depth), sizes.sent]
    if carried:
        aliases = {len(operands): len(outs) - 2}
        operands += (whole,)
        specs += [ANY]
    return run(
        body,
        f"adjoint_{step_no}",
        operands,
        specs,
        outs,
        [sizes.chain] + [sizes.pair] * 5,
        aliases,
    )


def forward_begin(sizes, wave, received):
    def body(w_ref, in_ref, c_out, z_out, c, sems):
        _, _, core = place()
        copies = Copies(sems)
        load_split(copies, sizes, w_ref.at[1, 0], in_ref, c)
        copies.wait()
        copies.start(c.at[core], z_out)
        copies.start(c, c_out)
        copies.wait()

    return run(
        body,
        "forward_begin",
        (wave, received),
        [ANY] * 2,
        [sizes.pair, sizes.block],
        [sizes.pair],
    )


def forward_step(sizes, step_no, current, other, beside, before, speed, later, gradient, source):
    split = isinstance(before, tuple)
    more = step_no < STEPS
    adds = gradient is not None
    n_before = (1 + split) if more else 0
    n_in = 5 + adds + n_before + 3 * more

    def body(*refs):
        c_ref, other_ref, beside_ref, v_ref, later_ref = refs[:5]
        g_ref = refs[5] if adds else None
        before_refs = refs[5 + adds : 5 + adds + n_before]
        rest = list(refs[n_in:])
        if more:
            cells_ref, wavelet_ref, start_ref = refs[n_in - 3 : n_in]
            next_out, z_out, g_out = rest[:3]
            rest = rest[3:]
        else:
            g_out, sent_out = rest[:2]
            rest = rest[2:]
        chain, mixed, late, last, v, g, sems = rest
        level, half, core = place()
        copies = Copies(sems)
        load_chain(copies, sizes, c_ref, other_ref, beside_ref, chain)
        copies.start(later_ref, late)
        copies.start(v_ref, v)
        if adds:
            copies.start(g_ref, g)
        if more:
            if split:
                load_split(copies, sizes, before_refs[0].at[0, 0], before_refs[1], last)
            else:
                copies.start(before_refs[0], last)
        copies.wait()
        differences(sizes, chain, mixed)

        def finish(slot, row, cut, centre, total):
            product = late[slot, row, cut, :] * total
            if adds:
                product = product + g[slot, row, cut, :]
            here = v[slot, row, cut, :]
            if more:
                g[slot, row, cut, :] = product
                last[slot, row, cut, :] = (
                    2.0 * centre - last[slot, row, cut, :] + here * here * total
                )
            else:
                g[slot, row, cut, :] = 2.0 * here * product

        sweep(sizes, chain, mixed, finish)
        if more:
            rows = sizes.rows
            along = cells_ref[0, 0] - level * (4 * rows) - core * rows
            col = cells_ref[0, 1] - half * (sizes.half - EXTRA)
            pulse = wavelet_ref[0, start_ref[0] + step_no]
            for slot in range(2):
                row = along - slot * 2 * rows

                @pl.when((row >= 0) & (row < rows) & (col >= 0) & (col < sizes.wide))
                def _():
                    depth_ids = lax.broadcasted_iota(jnp.int32, (1, sizes.depth), 1)
                    at = (slot, row, pl.ds(col, 1), slice(None))
                    last[at] = last[at] + jnp.where(depth_ids == cells_ref[0, 2], pulse, 0.0)

            copies.start(last.at[core], z_out)
            copies.start(last, next_out)
            copies.start(g, g_out)
        else:
            copies.start(g.at[1 - half, :, sizes.own(half), :], sent_out)
            copies.start(
                g.at[half, :, sizes.own(half), :], g_out.at[:, sizes.final(half), :]
            )
        copies.wait()

    operands = (current, other, beside, speed, later)
    if adds:
        operands += (gradient,)
    if more:
        operands += before if split else (before,)
    specs = [ANY] * len(operands)
    if more:
        operands += source
        specs += [SMEM] * 3
        outs = [sizes.pair, sizes.block, sizes.pair]
    else:
        outs = [(sizes.rows, sizes.cols, sizes.depth), sizes.sent]
    return run(
        body,
        f"forward_{step_no}",
        operands,
        specs,
        outs,
        [sizes.chain] + [sizes.pair] * 5,
    )


def fill(sizes, whole, received, name):
    shape = whole.shape

    def body(*refs):
        in_refs, out, sems = refs[: len(received)], refs[-2], refs[-1]
        _, half, _ = place()
        copies = Copies(sems)
        for index, ref in enumerate(in_refs):
            target = out.at[index, 0] if len(shape) == 5 else out
            copies.start(ref, target.at[:, sizes.final(1 - half), :])
        copies.wait()

    return run(
        body,
        name,
        (*received, whole),
        [ANY] * (len(received) + 1),
        [shape],
        [],
        {len(received): 0},
        flops=0,
    )[0]


def on_device(
    wave_state, adjoint_state, velocity, wavelet, traces, source_cells, receiver_cells, start_step
):
    count = lax.axis_size("gx")
    sizes = Sizes(*velocity.shape)
    across = [(i, i ^ 2) for i in range(count)]
    cores = [(i, i ^ 1) for i in range(count)]
    levels = []
    for level in range(count // 4 - 1):
        for half in range(2):
            low, high = 4 * level + 2 * half + 1, 4 * level + 4 + 2 * half
            levels += [(low, high), (high, low)]
    _, half, _ = place()
    start = start_step[0]
    recent = lax.dynamic_slice_in_dim(traces, start + 1, STEPS, 1)
    samples = lax.all_gather(recent, "gx", axis=2, tiled=True)

    def over(field):
        return lax.ppermute(field, "gx", across)

    def theirs(field):
        first = (1 - half) * (sizes.half - EXTRA)
        return over(lax.dynamic_slice_in_dim(field, first, sizes.wide, 1))

    def exchange(mine, edge):
        return lax.ppermute(mine, "gx", cores), lax.ppermute(edge, "gx", levels)

    velocity_in = theirs(velocity)
    later_in = theirs(adjoint_state[0, 0])
    latest_in = theirs(adjoint_state[1, 0])
    current_in = theirs(wave_state[1, 0])
    before_in = theirs(wave_state[0, 0])

    speed, later4, scaled, edge = adjoint_begin(
        sizes, velocity, velocity_in, adjoint_state, later_in
    )
    adjoint = functools.partial(adjoint_step, sizes)
    common = (speed, receiver_cells, samples)
    later3, scaled, edge = adjoint(
        4, scaled, *exchange(scaled, edge), later4, (adjoint_state, latest_in), *common, None
    )
    later2, scaled, edge = adjoint(
        3, scaled, *exchange(scaled, edge), later3, later4, *common, None
    )
    later1, scaled, edge, whole, sent1 = adjoint(
        2, scaled, *exchange(scaled, edge), later2, later3, *common, None
    )
    got1 = over(sent1)
    whole, sent0 = adjoint(
        1, scaled, *exchange(scaled, edge), later1, later2, *common, whole
    )
    got0 = over(sent0)

    forward = functools.partial(forward_step, sizes)
    source = (source_cells, wavelet, start_step)
    current1, edge = forward_begin(sizes, wave_state, current_in)
    current2, edge, gradient = forward(
        1, current1, *exchange(current1, edge), (wave_state, before_in), speed, later1, None, source
    )
    current3, edge, gradient = forward(
        2, current2, *exchange(current2, edge), current1, speed, later2, gradient, source
    )
    current4, edge, gradient = forward(
        3, current3, *exchange(current3, edge), current2, speed, later3, gradient, source
    )
    gradient, sent = forward(
        4, current4, *exchange(current4, edge), None, speed, later4, gradient, None
    )
    got = over(sent)
    return fill(sizes, gradient, [got], "fill_gradient"), fill(
        sizes, whole, [got0, got1], "fill_adjoint"
    )


def solution(mesh):
    in_specs = (
        P(None, "groups", "gx", None, None),
        P(None, "groups", "gx", None, None),
        P("gx", "groups", None),
        P("groups", None),
        P("groups", None, "gx"),
        P("groups", None),
        P("groups", None, None),
        P("groups"),
    )
    out_specs = (P("gx", "groups", None), P(None, "groups", "gx", None, None))
    return jax.shard_map(
        on_device, mesh=mesh, in_specs=in_specs, out_specs=out_specs, check_vma=False
    )
```

```python
import functools

import jax
import jax.numpy as jnp
from jax import lax
from jax.experimental import pallas as pl
from jax.experimental.pallas import tpu as pltpu
from jax.sharding import PartitionSpec as P

STEPS = 4
WEIGHTS = (-205.0 / 72.0, 8.0 / 5.0, -1.0 / 5.0, 8.0 / 315.0, -1.0 / 560.0)
UNIT = WEIGHTS[1]
REACH = 4
EXTRA = REACH * STEPS
F32 = jnp.float32
BF16 = jnp.bfloat16
ANY = pl.BlockSpec(memory_space=pl.ANY)
VMEM = pl.BlockSpec(memory_space=pltpu.VMEM)
SMEM = pl.BlockSpec(memory_space=pltpu.SMEM)
MIB = 2**20
PACK_LIMIT = 56


def place():
    position = lax.axis_index("gx")
    return position // 4, (position % 4) // 2, position % 2


def banded(apart):
    band = jnp.zeros(apart.shape, F32)
    for offset in range(1, REACH + 1):
        band = jnp.where(jnp.abs(apart) == offset, WEIGHTS[offset] / UNIT, band)
    return band.astype(BF16)


def iota(shape, axis):
    return lax.broadcasted_iota(jnp.int32, shape, axis)


def two_terms(value):
    high = value.astype(BF16)
    return high, (value - high.astype(F32)).astype(BF16)


def dot(left, right, contract=((1,), (0,))):
    return lax.dot_general(left, right, (contract, ((), ())), preferred_element_type=F32)


class Copies:
    def __init__(self, sems):
        self.sems, self.going = sems, []

    def start(self, source, target):
        copy = pltpu.make_async_copy(source, target, self.sems.at[len(self.going)])
        copy.start()
        self.going.append(copy)

    def wait(self):
        for copy in self.going:
            copy.wait()


class Sizes:
    def __init__(self, rows, cols, depth):
        self.rows, self.cols, self.depth = rows, cols, depth
        self.half = cols // 2
        self.wide = self.half + EXTRA
        self.pair = (2, rows, self.wide, depth)
        self.block = (rows, self.wide, depth)
        self.moved = (rows * self.wide + 8, depth)
        self.moved_first = (rows * self.wide + 16, depth)
        self.sent = (rows, self.half, depth)
        self.whole = (rows, cols, depth)

    def window(self, half):
        return pl.ds(pl.multiple_of(half * (self.half - EXTRA), 16), self.wide)

    def own(self, half):
        return pl.ds(pl.multiple_of(half * EXTRA, 16), self.half)

    def final(self, half):
        return pl.ds(pl.multiple_of(half * self.half, 16), self.half)

    def moved_row(self, row):
        return pl.ds(row * self.wide, self.wide)

    @property
    def moved_tail(self):
        return pl.ds(self.rows * self.wide, 16)


def over_columns(sizes, body):
    @pl.loop(0, sizes.wide // 16)
    def _(step):
        for part in range(2):
            body(pl.multiple_of(step * 16 + part * 8, 8))


def cut(first):
    return pl.ds(first, 8)


def merged(sizes, own, moved, slot, row, first):
    _, half, _ = place()
    received = moved[pl.ds(pl.multiple_of(first + row * sizes.wide, 8), 8), :]
    return jnp.where(half == slot, own[row, cut(first), :], received)


def differences(sizes, blocks, mixed, added=None):
    wide, depth = sizes.wide, sizes.depth
    shape = (wide, 2 * wide)
    column = iota(shape, 1)
    column = jnp.where(column >= wide, column - wide, column)
    band_y = banded(iota(shape, 0) - column)
    shape = (2 * depth, depth)
    layer = iota(shape, 0)
    layer = jnp.where(layer >= depth, layer - depth, layer)
    band_z = banded(layer - iota(shape, 1))
    for slot in range(2):
        for row in range(sizes.rows):
            terms = two_terms(blocks[slot][row])
            total = dot(jnp.concatenate(terms, 1), band_z)
            total = UNIT * (total + dot(band_y, jnp.concatenate(terms, 0)))
            if added is not None:
                total = total + added(slot, row)
            mixed[slot, row] = total


def sweep(sizes, refs, mixed, finish):
    mine0, mine1, other0, other1, beside = refs
    rows = sizes.rows
    _, _, core = place()
    orders = (
        (beside, mine0, other0, mine1, other1),
        (other0, mine0, other1, mine1, beside),
    )
    for which, order in enumerate(orders):

        @pl.when(core == which)
        def _():
            for slot in range(2):

                def columns(first):
                    near = [
                        block[row, cut(first), :]
                        for block in order[2 * slot : 2 * slot + 3]
                        for row in range(rows)
                    ]
                    for row in range(rows):
                        centre = near[rows + row]
                        parts = [
                            WEIGHTS[offset]
                            * (near[rows + row + offset] + near[rows + row - offset])
                            for offset in range(1, REACH + 1)
                        ]
                        total = (parts[0] + parts[1]) + (parts[2] + parts[3])
                        total = total + (
                            3.0 * WEIGHTS[0] * centre + mixed[slot, row, cut(first), :]
                        )
                        finish(which, slot, row, first, centre, total)

                over_columns(sizes, columns)


def run(body, name, operands, specs, outs, scratch=(), aliases=None, limit=24, sems=0):
    return pl.pallas_call(
        body,
        name=name,
        out_shape=[jax.ShapeDtypeStruct(shape, F32) for shape, _ in outs],
        in_specs=specs,
        out_specs=[spec for _, spec in outs],
        scratch_shapes=[pltpu.VMEM(shape, F32) for shape in scratch]
        + ([pltpu.SemaphoreType.DMA((sems,))] if sems else []),
        input_output_aliases=aliases or {},
        compiler_params=pltpu.CompilerParams(vmem_limit_bytes=limit * MIB),
        cost_estimate=pl.CostEstimate(flops=0, bytes_accessed=0, transcendentals=0),
    )(*operands)


def pack(sizes, velocity, adjoint, wave, traces):
    def body(v_ref, a_ref, w_ref, traces_ref, *rest):
        outs, sems = rest[:5], rest[5]
        _, half, _ = place()
        copies = Copies(sems)
        fields = (v_ref, a_ref.at[0, 0], a_ref.at[1, 0], w_ref.at[1, 0], w_ref.at[0, 0])
        for field, out in zip(fields, outs):
            for row in range(sizes.rows):
                copies.start(
                    field.at[row, sizes.window(1 - half), :], out.at[sizes.moved_row(row)]
                )
        each, steps = traces_ref.shape
        for out in outs[1:]:
            out[sizes.rows * sizes.wide :, :] = jnp.zeros((8, sizes.depth), F32)
        outs[0][sizes.rows * sizes.wide :, :] = jnp.zeros((16, sizes.depth), F32)
        outs[0][pl.ds(sizes.rows * sizes.wide, each), :steps] = traces_ref[...]
        copies.wait()

    return run(
        body,
        "pack",
        (velocity, adjoint, wave, traces),
        [ANY] * 3 + [VMEM],
        [(sizes.moved_first, VMEM)] + [(sizes.moved, VMEM)] * 4,
        limit=PACK_LIMIT,
        sems=20,
    )


def keep(sizes, velocity, adjoint, wave):
    def body(v_ref, a_ref, w_ref, *rest):
        outs, sems = rest[:5], rest[5]
        _, half, _ = place()
        copies = Copies(sems)
        fields = (v_ref, a_ref.at[0, 0], a_ref.at[1, 0], w_ref.at[1, 0], w_ref.at[0, 0])
        for field, out in zip(fields, outs):
            copies.start(field.at[:, sizes.window(half), :], out)
        copies.wait()

    return run(
        body,
        "keep",
        (velocity, adjoint, wave),
        [ANY] * 3,
        [(sizes.block, VMEM)] * 5,
        limit=PACK_LIMIT,
        sems=5,
    )


def speed_begin(sizes, own, moved, sent):
    def body(own_ref, moved_ref, sent_ref, v_out, tail_out):
        _, half, _ = place()
        tail_out[half] = sent_ref[sizes.moved_tail, :]
        tail_out[1 - half] = moved_ref[sizes.moved_tail, :]

        def columns(first):
            for slot in range(2):
                for row in range(sizes.rows):
                    v_out[slot, row, cut(first), :] = merged(
                        sizes, own_ref, moved_ref, slot, row, first
                    )

        over_columns(sizes, columns)

    return run(
        body,
        "speed_begin",
        (own, moved, sent),
        [VMEM] * 3,
        [(sizes.pair, VMEM), ((2, 16, sizes.depth), VMEM)],
    )


def adjoint_begin(sizes, speed, own, moved, settled):
    def body(v_ref, own_ref, moved_ref, _, a_out, u0_out, u1_out, z_out):
        _, _, core = place()

        def columns(first):
            for slot, u_out in enumerate((u0_out, u1_out)):
                for row in range(sizes.rows):
                    value = merged(sizes, own_ref, moved_ref, slot, row, first)
                    a_out[slot, row, cut(first), :] = value
                    here = v_ref[slot, row, cut(first), :]
                    u_out[row, cut(first), :] = here * here * value
            for row in range(sizes.rows):
                z_out[row, cut(first), :] = jnp.where(
                    core == 0, u0_out[row, cut(first), :], u1_out[row, cut(first), :]
                )

        over_columns(sizes, columns)

    return run(
        body,
        "adjoint_begin",
        (speed, own, moved, settled),
        [VMEM] * 3 + [ANY],
        [(sizes.pair, VMEM)] + [(sizes.block, VMEM)] * 3,
    )


def adjoint_step(sizes, step_no, scaled, later, latest, speed, cells, samples, settled=()):
    split = len(latest) == 2
    more = step_no > 1
    ends = step_no <= 2

    def body(*refs):
        refs = list(refs)
        u_refs, (later_ref, v_ref, cells_ref, samples_ref) = refs[:5], refs[5:9]
        latest_refs, refs = refs[9 : 9 + len(latest)], refs[9 + len(latest) + len(settled) :]
        if more:
            (next_out, u0_out, u1_out, z_out), refs = refs[:4], refs[4:]
        if ends:
            (kept_out, sent_out), refs = refs[:2], refs[2:]
        mixed = refs.pop(0)
        if not more:
            next_out = refs.pop(0)
        level, half, core = place()
        where_x, where_y, where_z = (cells_ref[0, axis : axis + 1, :] for axis in range(3))
        count = where_x.shape[1]
        values = jnp.where(
            where_z == iota((sizes.depth, count), 0),
            samples_ref[0, step_no - 1 : step_no, :],
            0.0,
        )
        values = jnp.concatenate(two_terms(values), 1)
        col_ids = iota((sizes.wide, count), 0) + half * (sizes.half - EXTRA)

        def added(slot, row):
            this_row = ((level * 2 + slot) * 2 + core) * sizes.rows + row
            col_of = jnp.where(where_x == this_row, where_y, -1)
            hit = jnp.where(col_of == col_ids, 1.0, 0.0).astype(BF16)
            return dot(jnp.concatenate((hit, hit), 1), values, ((1,), (1,)))

        differences(sizes, u_refs, mixed, added)

        def finish(which, slot, row, first, centre, total):
            at = (slot, row, cut(first), slice(None))
            if split:
                last = merged(sizes, *latest_refs, slot, row, first)
            else:
                last = latest_refs[0][at]
            value = 2.0 * later_ref[at] - last + total
            next_out[at] = value
            if more:
                here = v_ref[at]
                value = here * here * value
                (u0_out, u1_out)[slot][row, cut(first), :] = value
                if which == slot:
                    z_out[row, cut(first), :] = value

        sweep(sizes, u_refs, mixed, finish)
        if ends:
            kept_out[...] = next_out[half, :, sizes.own(half), :]
            sent_out[...] = next_out[1 - half, :, sizes.own(half), :]

    outs = []
    if more:
        outs += [(sizes.pair, VMEM)] + [(sizes.block, VMEM)] * 3
    if ends:
        outs += [(sizes.sent, VMEM)] * 2
    return run(
        body,
        f"adjoint_{step_no}",
        (*scaled, later, speed, cells, samples, *latest, *settled),
        [VMEM] * (9 + len(latest)) + [ANY] * len(settled),
        outs,
        [sizes.pair] * (1 if more else 2),
    )


def forward_begin(sizes, own, moved):
    def body(own_ref, moved_ref, c0_out, c1_out, z_out):
        _, _, core = place()

        def columns(first):
            for row in range(sizes.rows):
                pair = [merged(sizes, own_ref, moved_ref, slot, row, first) for slot in range(2)]
                c0_out[row, cut(first), :] = pair[0]
                c1_out[row, cut(first), :] = pair[1]
                z_out[row, cut(first), :] = jnp.where(core == 0, *pair)

        over_columns(sizes, columns)

    return run(
        body, "forward_begin", (own, moved), [VMEM] * 2, [(sizes.block, VMEM)] * 3
    )


def forward_step(sizes, step_no, current, before, speed, later, gradient, source, settled=()):
    first_step = step_no == 1
    more = step_no < STEPS

    def body(*refs):
        refs = list(refs)
        c_refs, v_ref, refs = refs[:5], refs[5], refs[6:]
        late, refs = refs[: len(later)], refs[len(later) :]
        if not first_step:
            g_ref, refs = refs[0], refs[1:]
        if more:
            before_refs, refs = refs[:2], refs[2:]
            (cells_ref, wavelet_ref, start_ref), refs = refs[:3], refs[3:]
        refs = refs[len(settled) :]
        if more:
            (c0_out, c1_out, z_out, g_out), refs = refs[:4], refs[4:]
        else:
            (kept_out, sent_out), refs = refs[:2], refs[2:]
        mixed = refs.pop(0)
        if not more:
            g_out = refs.pop(0)
        level, half, core = place()
        differences(sizes, c_refs, mixed)

        def finish(which, slot, row, first, centre, total):
            at = (slot, row, cut(first), slice(None))
            if first_step:
                g_out[at] = total
            elif step_no == 2:
                g_out[at] = late[0][at] * g_ref[at] + late[1][at] * total
            elif more:
                g_out[at] = g_ref[at] + late[0][at] * total
            else:
                g_out[at] = 2.0 * v_ref[at] * (g_ref[at] + late[0][at] * total)
            if more:
                if first_step:
                    last = merged(sizes, *before_refs, slot, row, first)
                else:
                    last = before_refs[slot][row, cut(first), :]
                here = v_ref[at]
                value = 2.0 * centre - last + here * here * total
                (c0_out, c1_out)[slot][row, cut(first), :] = value
                if which == slot:
                    z_out[row, cut(first), :] = value

        sweep(sizes, c_refs, mixed, finish)
        if not more:
            kept_out[...] = g_out[half, :, sizes.own(half), :]
            sent_out[...] = g_out[1 - half, :, sizes.own(half), :]
            return
        col = cells_ref[0, 1] - half * (sizes.half - EXTRA)
        pulse = wavelet_ref[0, start_ref[0] + step_no]
        for slot, c_out in enumerate((c0_out, c1_out)):
            row = cells_ref[0, 0] - ((level * 2 + slot) * 2 + core) * sizes.rows
            inside = (row >= 0) & (row < sizes.rows) & (col >= 0) & (col < sizes.wide)

            def put(out):
                at = (row, pl.ds(col, 1), slice(None))
                hit = iota((1, sizes.depth), 1) == cells_ref[0, 2]
                out[at] = out[at] + jnp.where(hit, pulse, 0.0)

            pl.when(inside)(functools.partial(put, c_out))
            pl.when(inside & (core == slot))(functools.partial(put, z_out))

    operands = (*current, speed, *later)
    if not first_step:
        operands += (gradient,)
    if more:
        operands += before
    specs = [VMEM] * len(operands)
    if more:
        operands += source
        specs += [SMEM] * 3
        outs = [(sizes.block, VMEM)] * 3 + [(sizes.pair, VMEM)]
    else:
        outs = [(sizes.sent, VMEM)] * 2
    return run(
        body,
        f"forward_{step_no}",
        (*operands, *settled),
        specs + [ANY] * len(settled),
        outs,
        [sizes.pair] * (1 if more else 2),
    )


def fill(sizes, shape, parts, name):
    def body(*refs):
        out, sems = refs[-2], refs[-1]
        _, half, _ = place()
        copies = Copies(sems)
        for index, ref in enumerate(refs[:-2]):
            target = out.at[index // 2, 0] if len(shape) == 5 else out
            side = half if index % 2 == 0 else 1 - half
            copies.start(ref, target.at[:, sizes.final(side), :])
        copies.wait()

    return run(
        body, name, parts, [ANY] * len(parts), [(shape, ANY)], sems=len(parts)
    )[0]


def on_device(
    wave_state, adjoint_state, velocity, wavelet, traces, source_cells, receiver_cells, start_step
):
    count = lax.axis_size("gx")
    sizes = Sizes(*velocity.shape)
    across = [(i, i ^ 2) for i in range(count)]
    cores = [(i, i ^ 1) for i in range(count)]
    levels = []
    for level in range(count // 4 - 1):
        for half in range(2):
            low, high = 4 * level + 2 * half + 1, 4 * level + 4 + 2 * half
            levels += [(low, high), (high, low)]
    halves = [[i for i in range(count) if (i % 4) // 2 == half] for half in range(2)]

    def over(field):
        return lax.ppermute(field, "gx", across)

    def exchange(block0, block1, edge):
        return (
            block0,
            block1,
            lax.ppermute(block0, "gx", cores),
            lax.ppermute(block1, "gx", cores),
            lax.ppermute(edge, "gx", levels),
        )

    each, steps = traces.shape[2], traces.shape[1]
    sent = pack(sizes, velocity, adjoint_state, wave_state, traces[0].T)
    velocity_in, later_in, latest_in, current_in, before_in = map(over, sent)
    kept = keep(sizes, velocity, adjoint_state, wave_state)

    speed, tails = speed_begin(sizes, kept[0], velocity_in, sent[0])
    tails = lax.all_gather(tails, "gx", axis_index_groups=halves)
    tails = tails[:, :, :each, :steps].reshape(count // 4, 2, 2, each, steps)
    samples = tails.transpose(4, 0, 2, 1, 3).reshape(1, steps, count * each)
    samples = lax.dynamic_slice_in_dim(samples, start_step[0] + 1, STEPS, 1)

    adjoint = functools.partial(adjoint_step, sizes)
    common = (speed, receiver_cells, samples)
    forward = functools.partial(forward_step, sizes)
    source = (source_cells, wavelet, start_step)
    later4, *scaled = adjoint_begin(sizes, speed, kept[1], later_in, samples)
    later3, *scaled = adjoint(4, exchange(*scaled), later4, (kept[2], latest_in), *common)
    current1 = forward_begin(sizes, kept[3], current_in)
    later2, *scaled = adjoint(3, exchange(*scaled), later3, (later4,), *common)
    scaled2 = exchange(*scaled)
    *current2, image = forward(
        1, exchange(*current1), (kept[4], before_in), speed, (), None, source, scaled2[2:]
    )
    later1, *scaled, mine1, sent1 = adjoint(
        2, scaled2, later2, (later3,), *common, tuple(current2[2:])
    )
    got1 = over(sent1)
    *current3, gradient = forward(
        2, exchange(*current2), tuple(current1[:2]), speed, (later1, later2), image, source
    )
    mine0, sent0 = adjoint(
        1, exchange(*scaled), later1, (later2,), *common, tuple(current3[2:])
    )
    got0 = over(sent0)
    *current4, gradient = forward(
        3,
        exchange(*current3),
        tuple(current2[:2]),
        speed,
        (later3,),
        gradient,
        source,
        (mine0, got1),
    )
    mine, sent = forward(4, exchange(*current4), (), speed, (later4,), gradient, None, (got0,))
    got = over(sent)
    return fill(sizes, sizes.whole, [mine, got], "fill_gradient"), fill(
        sizes, adjoint_state.shape, [mine0, got0, mine1, got1], "fill_adjoint"
    )


def solution(mesh):
    in_specs = (
        P(None, "groups", "gx", None, None),
        P(None, "groups", "gx", None, None),
        P("gx", "groups", None),
        P("groups", None),
        P("groups", None, "gx"),
        P("groups", None),
        P("groups", None, None),
        P("groups"),
    )
    out_specs = (P("gx", "groups", None), P(None, "groups", "gx", None, None))
    return jax.shard_map(
        on_device, mesh=mesh, in_specs=in_specs, out_specs=out_specs, check_vma=False
    )
```

```python
import functools

import jax
import jax.numpy as jnp
from jax import lax
from jax.experimental import pallas as pl
from jax.experimental.pallas import tpu as pltpu
from jax.sharding import PartitionSpec as P

STEPS = 4
WEIGHTS = (-205.0 / 72.0, 8.0 / 5.0, -1.0 / 5.0, 8.0 / 315.0, -1.0 / 560.0)
UNIT = WEIGHTS[1]
REACH = 4
EXTRA = REACH * STEPS
F32 = jnp.float32
BF16 = jnp.bfloat16
ANY = pl.BlockSpec(memory_space=pl.ANY)
VMEM = pl.BlockSpec(memory_space=pltpu.VMEM)
SMEM = pl.BlockSpec(memory_space=pltpu.SMEM)
MIB = 2**20
PACK_LIMIT = 56


def place():
    position = lax.axis_index("gx")
    return position // 4, (position % 4) // 2, position % 2


def banded(apart):
    band = jnp.zeros(apart.shape, F32)
    for offset in range(1, REACH + 1):
        band = jnp.where(jnp.abs(apart) == offset, WEIGHTS[offset] / UNIT, band)
    return band.astype(BF16)


def iota(shape, axis):
    return lax.broadcasted_iota(jnp.int32, shape, axis)


def two_terms(value):
    high = value.astype(BF16)
    return high, (value - high.astype(F32)).astype(BF16)


def dot(left, right, contract=((1,), (0,))):
    return lax.dot_general(left, right, (contract, ((), ())), preferred_element_type=F32)


class Copies:
    def __init__(self, sems):
        self.sems, self.going = sems, []

    def start(self, source, target):
        copy = pltpu.make_async_copy(source, target, self.sems.at[len(self.going)])
        copy.start()
        self.going.append(copy)

    def wait(self):
        for copy in self.going:
            copy.wait()


class Sizes:
    def __init__(self, rows, cols, depth):
        self.rows, self.cols, self.depth = rows, cols, depth
        self.half = cols // 2
        self.wide = self.half + EXTRA
        self.pair = (2, rows, self.wide, depth)
        self.block = (rows, self.wide, depth)
        self.edge = (rows * self.wide + 8, depth)
        self.moved = (rows * self.wide + 16, depth)
        self.sent = (rows, self.half, depth)
        self.whole = (rows, cols, depth)

    def window(self, half):
        return pl.ds(pl.multiple_of(half * (self.half - EXTRA), 16), self.wide)

    def own(self, half):
        return pl.ds(pl.multiple_of(half * EXTRA, 16), self.half)

    def final(self, half):
        return pl.ds(pl.multiple_of(half * self.half, 16), self.half)

    def moved_row(self, row):
        return pl.ds(row * self.wide, self.wide)

    @property
    def moved_tail(self):
        return pl.ds(self.rows * self.wide, 16)


def over_columns(sizes, body):
    @pl.loop(0, sizes.wide // 16)
    def _(step):
        for part in range(2):
            body(pl.multiple_of(step * 16 + part * 8, 8))


def cut(first):
    return pl.ds(first, 8)


def flat(sizes, row, first):
    return pl.ds(pl.multiple_of(first + row * sizes.wide, 8), 8), slice(None)


def merged(sizes, own, moved, slot, row, first):
    _, half, _ = place()
    received = moved[flat(sizes, row, first)]
    return jnp.where(half == slot, own[row, cut(first), :], received)


def differences(sizes, blocks, mixed, added=None):
    wide, depth = sizes.wide, sizes.depth
    shape = (wide, 2 * wide)
    column = iota(shape, 1)
    column = jnp.where(column >= wide, column - wide, column)
    band_y = banded(iota(shape, 0) - column)
    shape = (2 * depth, depth)
    layer = iota(shape, 0)
    layer = jnp.where(layer >= depth, layer - depth, layer)
    band_z = banded(layer - iota(shape, 1))
    for slot in range(2):
        for row in range(sizes.rows):
            terms = two_terms(blocks[slot][row])
            total = dot(jnp.concatenate(terms, 1), band_z)
            total = UNIT * (total + dot(band_y, jnp.concatenate(terms, 0)))
            if added is not None:
                total = total + added(slot, row)
            mixed[slot, row] = total


def sweep(sizes, refs, mixed, finish):
    mine0, mine1, other0, other1, beside = refs
    rows = sizes.rows
    _, _, core = place()
    orders = (
        (beside, mine0, other0, mine1, other1),
        (other0, mine0, other1, mine1, beside),
    )
    for which, order in enumerate(orders):

        @pl.when(core == which)
        def _():
            for slot in range(2):

                def columns(first):
                    near = [
                        block[
                            flat(sizes, row, first)
                            if block is beside
                            else (row, cut(first), slice(None))
                        ]
                        for block in order[2 * slot : 2 * slot + 3]
                        for row in range(rows)
                    ]
                    for row in range(rows):
                        centre = near[rows + row]
                        parts = [
                            WEIGHTS[offset]
                            * (near[rows + row + offset] + near[rows + row - offset])
                            for offset in range(1, REACH + 1)
                        ]
                        total = (parts[0] + parts[1]) + (parts[2] + parts[3])
                        total = total + (
                            3.0 * WEIGHTS[0] * centre + mixed[slot, row, cut(first), :]
                        )
                        finish(which, slot, row, first, centre, total)

                over_columns(sizes, columns)


def run(body, name, operands, specs, outs, scratch=(), aliases=None, limit=24, sems=0):
    return pl.pallas_call(
        body,
        name=name,
        out_shape=[jax.ShapeDtypeStruct(shape, F32) for shape, _ in outs],
        in_specs=specs,
        out_specs=[spec for _, spec in outs],
        scratch_shapes=[pltpu.VMEM(shape, F32) for shape in scratch]
        + ([pltpu.SemaphoreType.DMA((sems,))] if sems else []),
        input_output_aliases=aliases or {},
        compiler_params=pltpu.CompilerParams(vmem_limit_bytes=limit * MIB),
        cost_estimate=pl.CostEstimate(flops=0, bytes_accessed=0, transcendentals=0),
    )(*operands)


def pack_first(sizes, velocity, traces):
    def body(field, traces_ref, out, sems):
        _, half, _ = place()
        copies = Copies(sems)
        copies.start(
            field.at[:, sizes.window(1 - half), :],
            out.at[pl.ds(0, sizes.rows * sizes.wide)].reshape(sizes.block),
        )
        each, steps = traces_ref.shape
        out[sizes.moved_tail, :] = jnp.zeros((16, sizes.depth), F32)
        out[pl.ds(sizes.rows * sizes.wide, each), :steps] = traces_ref[...]
        copies.wait()

    return run(
        body,
        "pack_first",
        (velocity, traces),
        [ANY, VMEM],
        [(sizes.moved, VMEM)],
        limit=PACK_LIMIT,
        sems=1,
    )


def pack(sizes, adjoint, wave):
    def body(a_ref, w_ref, *rest):
        outs, sems = rest[:4], rest[4]
        _, half, _ = place()
        copies = Copies(sems)
        fields = (a_ref.at[0, 0], a_ref.at[1, 0], w_ref.at[1, 0], w_ref.at[0, 0])
        for field, out in zip(fields, outs):
            copies.start(
                field.at[:, sizes.window(1 - half), :],
                out.at[pl.ds(0, sizes.rows * sizes.wide)].reshape(sizes.block),
            )
            out[sizes.moved_tail, :] = jnp.zeros((16, sizes.depth), F32)
        copies.wait()

    return run(
        body,
        "pack",
        (adjoint, wave),
        [ANY] * 2,
        [(sizes.moved, VMEM)] * 4,
        limit=PACK_LIMIT,
        sems=4,
    )


def keep(sizes, velocity, adjoint, wave):
    def body(v_ref, a_ref, w_ref, *rest):
        outs, sems = rest[:5], rest[5]
        _, half, _ = place()
        copies = Copies(sems)
        fields = (v_ref, a_ref.at[0, 0], a_ref.at[1, 0], w_ref.at[1, 0], w_ref.at[0, 0])
        for field, out in zip(fields, outs):
            copies.start(field.at[:, sizes.window(half), :], out)
        copies.wait()

    return run(
        body,
        "keep",
        (velocity, adjoint, wave),
        [ANY] * 3,
        [(sizes.block, VMEM)] * 5,
        limit=PACK_LIMIT,
        sems=5,
    )


def speed_begin(sizes, own, moved, sent):
    def body(own_ref, moved_ref, sent_ref, v_out, tail_out):
        _, half, _ = place()
        tail_out[half] = sent_ref[sizes.moved_tail, :]
        tail_out[1 - half] = moved_ref[sizes.moved_tail, :]

        def columns(first):
            for slot in range(2):
                for row in range(sizes.rows):
                    v_out[slot, row, cut(first), :] = merged(
                        sizes, own_ref, moved_ref, slot, row, first
                    )

        over_columns(sizes, columns)

    return run(
        body,
        "speed_begin",
        (own, moved, sent),
        [VMEM] * 3,
        [(sizes.pair, VMEM), ((2, 16, sizes.depth), VMEM)],
    )


def adjoint_begin(sizes, speed, own, moved, settled):
    def body(v_ref, own_ref, moved_ref, _, a_out, u0_out, u1_out, z_out):
        _, _, core = place()

        def columns(first):
            for slot, u_out in enumerate((u0_out, u1_out)):
                for row in range(sizes.rows):
                    value = merged(sizes, own_ref, moved_ref, slot, row, first)
                    a_out[slot, row, cut(first), :] = value
                    here = v_ref[slot, row, cut(first), :]
                    u_out[row, cut(first), :] = here * here * value
            for row in range(sizes.rows):
                z_out[flat(sizes, row, first)] = jnp.where(
                    core == 0, u0_out[row, cut(first), :], u1_out[row, cut(first), :]
                )

        over_columns(sizes, columns)

    return run(
        body,
        "adjoint_begin",
        (speed, own, moved, settled),
        [VMEM] * 3 + [ANY],
        [(sizes.pair, VMEM)] + [(sizes.block, VMEM)] * 2 + [(sizes.edge, VMEM)],
    )


def adjoint_step(sizes, step_no, scaled, later, latest, speed, cells, samples, settled=()):
    split = len(latest) == 2
    more = step_no > 1
    ends = step_no <= 2

    def body(*refs):
        refs = list(refs)
        u_refs, (later_ref, v_ref, cells_ref, samples_ref) = refs[:5], refs[5:9]
        latest_refs, refs = refs[9 : 9 + len(latest)], refs[9 + len(latest) + len(settled) :]
        if more:
            (next_out, u0_out, u1_out, z_out), refs = refs[:4], refs[4:]
        if ends:
            (kept_out, sent_out), refs = refs[:2], refs[2:]
        mixed = refs.pop(0)
        if not more:
            next_out = refs.pop(0)
        level, half, core = place()
        where_x, where_y, where_z = (cells_ref[0, axis : axis + 1, :] for axis in range(3))
        count = where_x.shape[1]
        values = jnp.where(
            where_z == iota((sizes.depth, count), 0),
            samples_ref[0, step_no - 1 : step_no, :],
            0.0,
        )
        values = jnp.concatenate(two_terms(values), 1)
        col_ids = iota((sizes.wide, count), 0) + half * (sizes.half - EXTRA)

        def added(slot, row):
            this_row = ((level * 2 + slot) * 2 + core) * sizes.rows + row
            col_of = jnp.where(where_x == this_row, where_y, -1)
            hit = jnp.where(col_of == col_ids, 1.0, 0.0).astype(BF16)
            return dot(jnp.concatenate((hit, hit), 1), values, ((1,), (1,)))

        differences(sizes, u_refs, mixed, added)

        def finish(which, slot, row, first, centre, total):
            at = (slot, row, cut(first), slice(None))
            if split:
                last = merged(sizes, *latest_refs, slot, row, first)
            else:
                last = latest_refs[0][at]
            value = 2.0 * later_ref[at] - last + total
            next_out[at] = value
            if more:
                here = v_ref[at]
                value = here * here * value
                (u0_out, u1_out)[slot][row, cut(first), :] = value
                if which == slot:
                    z_out[flat(sizes, row, first)] = value

        sweep(sizes, u_refs, mixed, finish)
        if ends:
            kept_out[...] = next_out[half, :, sizes.own(half), :]
            for row in range(sizes.rows):
                sent_out[pl.ds(row * sizes.half, sizes.half), :] = next_out[
                    1 - half, row, sizes.own(half), :
                ]
            rest = sizes.moved[0] - sizes.rows * sizes.half
            sent_out[pl.ds(sizes.rows * sizes.half, rest), :] = jnp.zeros((rest, sizes.depth), F32)

    outs = []
    if more:
        outs += [(sizes.pair, VMEM)] + [(sizes.block, VMEM)] * 2 + [(sizes.edge, VMEM)]
    if ends:
        outs += [(sizes.sent, VMEM), (sizes.moved, VMEM)]
    return run(
        body,
        f"adjoint_{step_no}",
        (*scaled, later, speed, cells, samples, *latest, *settled),
        [VMEM] * (9 + len(latest)) + [ANY] * len(settled),
        outs,
        [sizes.pair] * (1 if more else 2),
    )


def forward_begin(sizes, own, moved, settled):
    def body(own_ref, moved_ref, *rest):
        c0_out, c1_out, z_out = rest[len(settled) :]
        _, _, core = place()

        def columns(first):
            for row in range(sizes.rows):
                pair = [merged(sizes, own_ref, moved_ref, slot, row, first) for slot in range(2)]
                c0_out[row, cut(first), :] = pair[0]
                c1_out[row, cut(first), :] = pair[1]
                z_out[flat(sizes, row, first)] = jnp.where(core == 0, *pair)

        over_columns(sizes, columns)

    return run(
        body,
        "forward_begin",
        (own, moved, *settled),
        [VMEM] * 2 + [ANY] * len(settled),
        [(sizes.block, VMEM)] * 2 + [(sizes.edge, VMEM)],
    )


def forward_step(sizes, step_no, current, before, speed, later, gradient, source, settled=()):
    first_step = step_no == 1
    more = step_no < STEPS

    def body(*refs):
        refs = list(refs)
        c_refs, v_ref, refs = refs[:5], refs[5], refs[6:]
        late, refs = refs[: len(later)], refs[len(later) :]
        if not first_step:
            g_ref, refs = refs[0], refs[1:]
        if more:
            before_refs, refs = refs[:2], refs[2:]
            (cells_ref, wavelet_ref, start_ref), refs = refs[:3], refs[3:]
        refs = refs[len(settled) :]
        if more:
            (c0_out, c1_out, z_out, g_out), refs = refs[:4], refs[4:]
        else:
            (kept_out, sent_out), refs = refs[:2], refs[2:]
        mixed = refs.pop(0)
        if not more:
            g_out = refs.pop(0)
        level, half, core = place()
        differences(sizes, c_refs, mixed)

        def finish(which, slot, row, first, centre, total):
            at = (slot, row, cut(first), slice(None))
            if first_step:
                g_out[at] = total
            elif step_no == 2:
                g_out[at] = late[0][at] * g_ref[at] + late[1][at] * total
            elif more:
                g_out[at] = g_ref[at] + late[0][at] * total
            else:
                g_out[at] = 2.0 * v_ref[at] * (g_ref[at] + late[0][at] * total)
            if more:
                if first_step:
                    last = merged(sizes, *before_refs, slot, row, first)
                else:
                    last = before_refs[slot][row, cut(first), :]
                here = v_ref[at]
                value = 2.0 * centre - last + here * here * total
                (c0_out, c1_out)[slot][row, cut(first), :] = value
                if which == slot:
                    z_out[flat(sizes, row, first)] = value

        sweep(sizes, c_refs, mixed, finish)
        if not more:
            kept_out[...] = g_out[half, :, sizes.own(half), :]
            sent_out[...] = g_out[1 - half, :, sizes.own(half), :]
            return
        col = cells_ref[0, 1] - half * (sizes.half - EXTRA)
        pulse = wavelet_ref[0, start_ref[0] + step_no]
        for slot, c_out in enumerate((c0_out, c1_out)):
            row = cells_ref[0, 0] - ((level * 2 + slot) * 2 + core) * sizes.rows
            inside = (row >= 0) & (row < sizes.rows) & (col >= 0) & (col < sizes.wide)

            def put(out, at):
                hit = iota((1, sizes.depth), 1) == cells_ref[0, 2]
                out[at] = out[at] + jnp.where(hit, pulse, 0.0)

            pl.when(inside)(functools.partial(put, c_out, (row, pl.ds(col, 1), slice(None))))
            pl.when(inside & (core == slot))(
                functools.partial(put, z_out, (pl.ds(col + row * sizes.wide, 1), slice(None)))
            )

    operands = (*current, speed, *later)
    if not first_step:
        operands += (gradient,)
    if more:
        operands += before
    specs = [VMEM] * len(operands)
    if more:
        operands += source
        specs += [SMEM] * 3
        outs = [(sizes.block, VMEM)] * 2 + [(sizes.edge, VMEM), (sizes.pair, VMEM)]
    else:
        outs = [(sizes.sent, VMEM)] * 2
    return run(
        body,
        f"forward_{step_no}",
        (*operands, *settled),
        specs + [ANY] * len(settled),
        outs,
        [sizes.pair] * (1 if more else 2),
    )


def fill(sizes, shape, parts, name):
    def body(*refs):
        out, sems = refs[-2], refs[-1]
        _, half, _ = place()
        copies = Copies(sems)
        for index, ref in enumerate(refs[:-2]):
            target = out.at[index // 2, 0] if len(shape) == 5 else out
            side = half if index % 2 == 0 else 1 - half
            if len(ref.shape) == 2:
                ref = ref.at[pl.ds(0, sizes.rows * sizes.half)].reshape(sizes.sent)
            copies.start(ref, target.at[:, sizes.final(side), :])
        copies.wait()

    return run(
        body, name, parts, [ANY] * len(parts), [(shape, ANY)], sems=len(parts)
    )[0]


def on_device(
    wave_state, adjoint_state, velocity, wavelet, traces, source_cells, receiver_cells, start_step
):
    count = lax.axis_size("gx")
    sizes = Sizes(*velocity.shape)
    across = [(i, i ^ 2) for i in range(count)]
    cores = [(i, i ^ 1) for i in range(count)]
    levels = []
    for level in range(count // 4 - 1):
        for half in range(2):
            low, high = 4 * level + 2 * half + 1, 4 * level + 4 + 2 * half
            levels += [(low, high), (high, low)]
    halves = [[i for i in range(count) if (i % 4) // 2 == half] for half in range(2)]

    def over(field):
        return lax.ppermute(field, "gx", across)

    def exchange(block0, block1, edge):
        return (
            block0,
            block1,
            lax.ppermute(block0, "gx", cores),
            lax.ppermute(block1, "gx", cores),
            lax.ppermute(edge, "gx", levels),
        )

    each, steps = traces.shape[2], traces.shape[1]
    sent = pack_first(sizes, velocity, traces[0].T) + pack(sizes, adjoint_state, wave_state)
    velocity_in, later_in, latest_in, current_in, before_in = map(over, sent)
    kept = keep(sizes, velocity, adjoint_state, wave_state)

    speed, tails = speed_begin(sizes, kept[0], velocity_in, sent[0])
    tails = lax.all_gather(tails, "gx", axis_index_groups=halves)
    tails = tails[:, :, :each, :steps].reshape(count // 4, 2, 2, each, steps)
    samples = tails.transpose(4, 0, 2, 1, 3).reshape(1, steps, count * each)
    samples = lax.dynamic_slice_in_dim(samples, start_step[0] + 1, STEPS, 1)

    adjoint = functools.partial(adjoint_step, sizes)
    common = (speed, receiver_cells, samples)
    forward = functools.partial(forward_step, sizes)
    source = (source_cells, wavelet, start_step)
    later4, *scaled = adjoint_begin(sizes, speed, kept[1], later_in, samples)
    later3, *scaled = adjoint(4, exchange(*scaled), later4, (kept[2], latest_in), *common)
    scaled = exchange(*scaled)
    current1 = exchange(*forward_begin(sizes, kept[3], current_in, scaled[:1]))
    later2, *scaled = adjoint(3, scaled, later3, (later4,), *common, current1[:1])
    scaled = exchange(*scaled)
    *current2, image = forward(
        1, current1, (kept[4], before_in), speed, (), None, source
    )
    current2 = exchange(*current2)
    later1, *scaled, mine1, sent1 = adjoint(
        2, scaled, later2, (later3,), *common, current2[:1]
    )
    got1 = over(sent1)
    scaled = exchange(*scaled)
    *current3, gradient = forward(
        2, current2, current1[:2], speed, (later1, later2), image, source, scaled[2:4]
    )
    current3 = exchange(*current3)
    mine0, sent0 = adjoint(
        1, scaled, later1, (later2,), *common, current3[2:4]
    )
    got0 = over(sent0)
    *current4, gradient = forward(
        3, current3, current2[:2], speed, (later3,), gradient, source, (mine0, got1)
    )
    mine, sent = forward(4, exchange(*current4), (), speed, (later4,), gradient, None, (got0,))
    got = over(sent)
    return fill(sizes, sizes.whole, [mine, got], "fill_gradient"), fill(
        sizes, adjoint_state.shape, [mine0, got0, mine1, got1], "fill_adjoint"
    )


def solution(mesh):
    in_specs = (
        P(None, "groups", "gx", None, None),
        P(None, "groups", "gx", None, None),
        P("gx", "groups", None),
        P("groups", None),
        P("groups", None, "gx"),
        P("groups", None),
        P("groups", None, None),
        P("groups"),
    )
    out_specs = (P("gx", "groups", None), P(None, "groups", "gx", None, None))
    return jax.shard_map(
        on_device, mesh=mesh, in_specs=in_specs, out_specs=out_specs, check_vma=False
    )
```

```python
import functools

import jax
import jax.numpy as jnp
from jax import lax
from jax.experimental import pallas as pl
from jax.experimental.pallas import tpu as pltpu
from jax.sharding import PartitionSpec as P

STEPS = 4
WEIGHTS = (-205.0 / 72.0, 8.0 / 5.0, -1.0 / 5.0, 8.0 / 315.0, -1.0 / 560.0)
UNIT = WEIGHTS[1]
REACH = 4
EXTRA = REACH * STEPS
F32 = jnp.float32
BF16 = jnp.bfloat16
ANY = pl.BlockSpec(memory_space=pl.ANY)
VMEM = pl.BlockSpec(memory_space=pltpu.VMEM)
SMEM = pl.BlockSpec(memory_space=pltpu.SMEM)
MIB = 2**20
PACK_LIMIT = 56


def place():
    position = lax.axis_index("gx")
    return position // 4, (position % 4) // 2, position % 2


def banded(apart):
    band = jnp.zeros(apart.shape, F32)
    for offset in range(1, REACH + 1):
        band = jnp.where(jnp.abs(apart) == offset, WEIGHTS[offset] / UNIT, band)
    return band.astype(BF16)


def iota(shape, axis):
    return lax.broadcasted_iota(jnp.int32, shape, axis)


def two_terms(value):
    high = value.astype(BF16)
    return high, (value - high.astype(F32)).astype(BF16)


def dot(left, right, contract=((1,), (0,))):
    return lax.dot_general(left, right, (contract, ((), ())), preferred_element_type=F32)


class Copies:
    def __init__(self, sems):
        self.sems, self.going = sems, []

    def start(self, source, target):
        copy = pltpu.make_async_copy(source, target, self.sems.at[len(self.going)])
        copy.start()
        self.going.append(copy)

    def wait(self):
        for copy in self.going:
            copy.wait()


class Sizes:
    def __init__(self, rows, cols, depth):
        self.rows, self.cols, self.depth = rows, cols, depth
        self.half = cols // 2
        self.wide = self.half + EXTRA
        self.pair = (2, rows, self.wide, depth)
        self.block = (rows, self.wide, depth)
        self.edge = (rows * self.wide + 8, depth)
        self.moved = (rows * self.wide + 16, depth)
        self.sent = (rows, self.half, depth)
        self.whole = (rows, cols, depth)
        self.quarter = cols // 4
        self.quarters = (rows, self.quarter, depth)
        self.edges = (rows * self.quarter, depth)

    def window(self, half):
        return pl.ds(pl.multiple_of(half * (self.half - EXTRA), 16), self.wide)

    def own(self, half):
        return pl.ds(pl.multiple_of(half * EXTRA, 16), self.half)

    def final(self, half):
        return pl.ds(pl.multiple_of(half * self.half, 16), self.half)

    def moved_row(self, row):
        return pl.ds(row * self.wide, self.wide)

    @property
    def moved_tail(self):
        return pl.ds(self.rows * self.wide, 16)


def over_columns(sizes, body):
    @pl.loop(0, sizes.wide // 16)
    def _(step):
        for part in range(2):
            body(pl.multiple_of(step * 16 + part * 8, 8))


def cut(first):
    return pl.ds(first, 8)


def flat(sizes, row, first):
    return pl.ds(pl.multiple_of(first + row * sizes.wide, 8), 8), slice(None)


def merged(sizes, own, moved, slot, row, first):
    _, half, _ = place()
    received = moved[flat(sizes, row, first)]
    return jnp.where(half == slot, own[row, cut(first), :], received)


def differences(sizes, blocks, mixed, added=None):
    wide, depth = sizes.wide, sizes.depth
    shape = (wide, 2 * wide)
    column = iota(shape, 1)
    column = jnp.where(column >= wide, column - wide, column)
    band_y = banded(iota(shape, 0) - column)
    shape = (2 * depth, depth)
    layer = iota(shape, 0)
    layer = jnp.where(layer >= depth, layer - depth, layer)
    band_z = banded(layer - iota(shape, 1))
    for slot in range(2):
        for row in range(sizes.rows):
            terms = two_terms(blocks[slot][row])
            total = dot(jnp.concatenate(terms, 1), band_z)
            total = UNIT * (total + dot(band_y, jnp.concatenate(terms, 0)))
            if added is not None:
                total = total + added(slot, row)
            mixed[slot, row] = total


def along_rows(sizes, blocks, mixed, partial):
    mine0, mine1, other0, other1 = blocks
    rows = sizes.rows
    _, _, core = place()
    orders = (
        (None, mine0, other0, mine1, other1),
        (other0, mine0, other1, mine1, None),
    )
    for which, order in enumerate(orders):

        @pl.when(core == which)
        def _():
            for slot in range(2):

                def columns(first):
                    near = [
                        None if block is None else block[row, cut(first), :]
                        for block in order[2 * slot : 2 * slot + 3]
                        for row in range(rows)
                    ]
                    for row in range(rows):
                        parts = []
                        for offset in range(1, REACH + 1):
                            pair = (near[rows + row + offset], near[rows + row - offset])
                            pair = [value for value in pair if value is not None]
                            if pair:
                                parts.append(WEIGHTS[offset] * sum(pair[1:], pair[0]))
                        total = 3.0 * WEIGHTS[0] * near[rows + row]
                        total = total + mixed[slot, row, cut(first), :]
                        partial[slot, row, cut(first), :] = sum(parts[1:], parts[0]) + total

                over_columns(sizes, columns)


def prepare(sizes, blocks, name, inject=None, settled=()):
    def body(*refs):
        b_refs = refs[:4]
        partial, mixed = refs[-2:]
        added = None
        if inject is not None:
            step_no = inject[0]
            cells_ref, samples_ref = refs[4:6]
            level, half, core = place()
            where_x, where_y, where_z = (cells_ref[0, axis : axis + 1, :] for axis in range(3))
            count = where_x.shape[1]
            values = jnp.where(
                where_z == iota((sizes.depth, count), 0),
                samples_ref[0, step_no - 1 : step_no, :],
                0.0,
            )
            values = jnp.concatenate(two_terms(values), 1)
            col_ids = iota((sizes.wide, count), 0) + half * (sizes.half - EXTRA)

            def added(slot, row):
                this_row = ((level * 2 + slot) * 2 + core) * sizes.rows + row
                col_of = jnp.where(where_x == this_row, where_y, -1)
                hit = jnp.where(col_of == col_ids, 1.0, 0.0).astype(BF16)
                return dot(jnp.concatenate((hit, hit), 1), values, ((1,), (1,)))

        differences(sizes, b_refs, mixed, added)
        along_rows(sizes, b_refs, mixed, partial)

    operands = (*blocks, *(inject[1:] if inject is not None else ()))
    specs = [VMEM] * len(operands) + [ANY] * len(settled)
    return run(
        body,
        name,
        (*operands, *settled),
        specs,
        [(sizes.pair, VMEM)],
        [sizes.pair],
    )[0]


def sweep(sizes, partial, beside, finish):
    rows = sizes.rows
    _, _, core = place()
    for which in range(2):

        @pl.when(core == which)
        def _():
            def columns(first):
                far = [beside[flat(sizes, row, first)] for row in range(rows)]
                for slot in range(2):
                    for row in range(rows):
                        total = partial[slot, row, cut(first), :]
                        for offset in range(1, REACH + 1):
                            at = row + offset - rows if which else row - offset + rows
                            if slot == which and 0 <= at < rows:
                                total = total + WEIGHTS[offset] * far[at]
                        finish(which, slot, row, first, total)

            over_columns(sizes, columns)


def run(body, name, operands, specs, outs, scratch=(), aliases=None, limit=24, sems=0):
    return pl.pallas_call(
        body,
        name=name,
        out_shape=[jax.ShapeDtypeStruct(shape, F32) for shape, _ in outs],
        in_specs=specs,
        out_specs=[spec for _, spec in outs],
        scratch_shapes=[pltpu.VMEM(shape, F32) for shape in scratch]
        + ([pltpu.SemaphoreType.DMA((sems,))] if sems else []),
        input_output_aliases=aliases or {},
        compiler_params=pltpu.CompilerParams(vmem_limit_bytes=limit * MIB),
        cost_estimate=pl.CostEstimate(flops=0, bytes_accessed=0, transcendentals=0),
    )(*operands)


def pack_first(sizes, velocity, traces):
    def body(field, traces_ref, out, sems):
        _, half, _ = place()
        copies = Copies(sems)
        copies.start(
            field.at[:, sizes.window(1 - half), :],
            out.at[pl.ds(0, sizes.rows * sizes.wide)].reshape(sizes.block),
        )
        each, steps = traces_ref.shape
        out[sizes.moved_tail, :] = jnp.zeros((16, sizes.depth), F32)
        out[pl.ds(sizes.rows * sizes.wide, each), :steps] = traces_ref[...]
        copies.wait()

    return run(
        body,
        "pack_first",
        (velocity, traces),
        [ANY, VMEM],
        [(sizes.moved, VMEM)],
        limit=16,
        sems=1,
    )


def pack(sizes, adjoint, wave):
    def body(a_ref, w_ref, *rest):
        outs, sems = rest[:4], rest[4]
        _, half, _ = place()
        copies = Copies(sems)
        fields = (a_ref.at[0, 0], a_ref.at[1, 0], w_ref.at[1, 0], w_ref.at[0, 0])
        for field, out in zip(fields, outs):
            copies.start(
                field.at[:, sizes.window(1 - half), :],
                out.at[pl.ds(0, sizes.rows * sizes.wide)].reshape(sizes.block),
            )
            out[sizes.moved_tail, :] = jnp.zeros((16, sizes.depth), F32)
        copies.wait()

    return run(
        body,
        "pack",
        (adjoint, wave),
        [ANY] * 2,
        [(sizes.moved, VMEM)] * 4,
        limit=PACK_LIMIT,
        sems=4,
    )


def keep(sizes, velocity, adjoint, wave):
    def body(v_ref, a_ref, w_ref, *rest):
        outs, sems = rest[:5], rest[5]
        _, half, _ = place()
        copies = Copies(sems)
        fields = (v_ref, a_ref.at[0, 0], a_ref.at[1, 0], w_ref.at[1, 0], w_ref.at[0, 0])
        for field, out in zip(fields, outs):
            copies.start(field.at[:, sizes.window(half), :], out)
        copies.wait()

    return run(
        body,
        "keep",
        (velocity, adjoint, wave),
        [ANY] * 3,
        [(sizes.block, VMEM)] * 5,
        limit=PACK_LIMIT,
        sems=5,
    )


def speed_begin(sizes, own, moved, sent):
    def body(own_ref, moved_ref, sent_ref, v_out, tail_out):
        _, half, _ = place()
        tail_out[half] = sent_ref[sizes.moved_tail, :]
        tail_out[1 - half] = moved_ref[sizes.moved_tail, :]

        def columns(first):
            for slot in range(2):
                for row in range(sizes.rows):
                    v_out[slot, row, cut(first), :] = merged(
                        sizes, own_ref, moved_ref, slot, row, first
                    )

        over_columns(sizes, columns)

    return run(
        body,
        "speed_begin",
        (own, moved, sent),
        [VMEM] * 3,
        [(sizes.pair, VMEM), ((2, 16, sizes.depth), VMEM)],
    )


def adjoint_begin(sizes, speed, own, moved, settled):
    def body(v_ref, own_ref, moved_ref, _, a_out, u0_out, u1_out, z_out):
        _, _, core = place()

        def columns(first):
            for slot, u_out in enumerate((u0_out, u1_out)):
                for row in range(sizes.rows):
                    value = merged(sizes, own_ref, moved_ref, slot, row, first)
                    a_out[slot, row, cut(first), :] = value
                    here = v_ref[slot, row, cut(first), :]
                    u_out[row, cut(first), :] = here * here * value
            for row in range(sizes.rows):
                z_out[flat(sizes, row, first)] = jnp.where(
                    core == 0, u0_out[row, cut(first), :], u1_out[row, cut(first), :]
                )

        over_columns(sizes, columns)

    return run(
        body,
        "adjoint_begin",
        (speed, own, moved, settled),
        [VMEM] * 3 + [ANY],
        [(sizes.pair, VMEM)] + [(sizes.block, VMEM)] * 2 + [(sizes.edge, VMEM)],
    )


def adjoint_step(sizes, step_no, partial, beside, later, latest, speed, settled=()):
    split = len(latest) == 2
    more = step_no > 1
    ends = step_no <= 2

    def body(*refs):
        refs = list(refs)
        partial_ref, beside_ref, later_ref, v_ref = refs[:4]
        latest_refs, refs = refs[4 : 4 + len(latest)], refs[4 + len(latest) + len(settled) :]
        if more:
            (next_out, u0_out, u1_out, z_out), refs = refs[:4], refs[4:]
        if ends:
            (kept_out, sent_out), refs = refs[:2], refs[2:]
        if not more:
            next_out = refs.pop(0)
        _, half, _ = place()

        def finish(which, slot, row, first, total):
            at = (slot, row, cut(first), slice(None))
            if split:
                last = merged(sizes, *latest_refs, slot, row, first)
            else:
                last = latest_refs[0][at]
            value = 2.0 * later_ref[at] - last + total
            next_out[at] = value
            if more:
                here = v_ref[at]
                value = here * here * value
                (u0_out, u1_out)[slot][row, cut(first), :] = value
                if which == slot:
                    z_out[flat(sizes, row, first)] = value

        sweep(sizes, partial_ref, beside_ref, finish)
        if ends:
            kept_out[...] = next_out[half, :, sizes.own(half), :]
            for row in range(sizes.rows):
                sent_out[pl.ds(row * sizes.half, sizes.half), :] = next_out[
                    1 - half, row, sizes.own(half), :
                ]
            rest = sizes.moved[0] - sizes.rows * sizes.half
            sent_out[pl.ds(sizes.rows * sizes.half, rest), :] = jnp.zeros((rest, sizes.depth), F32)

    outs = []
    if more:
        outs += [(sizes.pair, VMEM)] + [(sizes.block, VMEM)] * 2 + [(sizes.edge, VMEM)]
    if ends:
        outs += [(sizes.sent, VMEM), (sizes.moved, VMEM)]
    return run(
        body,
        f"adjoint_{step_no}",
        (partial, beside, later, speed, *latest, *settled),
        [VMEM] * (4 + len(latest)) + [ANY] * len(settled),
        outs,
        [] if more else [sizes.pair],
    )


def forward_begin(sizes, own, moved, settled):
    def body(own_ref, moved_ref, *rest):
        c0_out, c1_out, z_out = rest[len(settled) :]
        _, _, core = place()

        def columns(first):
            for row in range(sizes.rows):
                pair = [merged(sizes, own_ref, moved_ref, slot, row, first) for slot in range(2)]
                c0_out[row, cut(first), :] = pair[0]
                c1_out[row, cut(first), :] = pair[1]
                z_out[flat(sizes, row, first)] = jnp.where(core == 0, *pair)

        over_columns(sizes, columns)

    return run(
        body,
        "forward_begin",
        (own, moved, *settled),
        [VMEM] * 2 + [ANY] * len(settled),
        [(sizes.block, VMEM)] * 2 + [(sizes.edge, VMEM)],
    )


def forward_step(
    sizes, step_no, partial, current, before, speed, later, gradient, source, settled=()
):
    first_step = step_no == 1
    last_step = step_no == STEPS - 1

    def body(*refs):
        refs = list(refs)
        partial_ref, c_refs, beside_ref, v_ref, refs = refs[0], refs[1:3], refs[3], refs[4], refs[5:]
        late, refs = refs[: len(later)], refs[len(later) :]
        if not first_step:
            g_ref, refs = refs[0], refs[1:]
        before_refs, refs = refs[:2], refs[2:]
        (cells_ref, wavelet_ref, start_ref), refs = refs[:3], refs[3:]
        c0_out, c1_out, g_out, *z_outs = refs[len(settled) :]
        level, half, core = place()

        def finish(which, slot, row, first, total):
            at = (slot, row, cut(first), slice(None))
            if first_step:
                g_out[at] = total
            elif step_no == 2:
                g_out[at] = late[0][at] * g_ref[at] + late[1][at] * total
            else:
                g_out[at] = g_ref[at] + late[0][at] * total
            if first_step:
                last = merged(sizes, *before_refs, slot, row, first)
            else:
                last = before_refs[slot][row, cut(first), :]
            here = v_ref[at]
            centre = c_refs[slot][row, cut(first), :]
            value = 2.0 * centre - last + here * here * total
            (c0_out, c1_out)[slot][row, cut(first), :] = value
            if which == slot and not last_step:
                z_outs[0][flat(sizes, row, first)] = value

        sweep(sizes, partial_ref, beside_ref, finish)
        col = cells_ref[0, 1] - half * (sizes.half - EXTRA)
        pulse = wavelet_ref[0, start_ref[0] + step_no]
        for slot, c_out in enumerate((c0_out, c1_out)):
            row = cells_ref[0, 0] - ((level * 2 + slot) * 2 + core) * sizes.rows
            inside = (row >= 0) & (row < sizes.rows) & (col >= 0) & (col < sizes.wide)

            def put(out, at):
                hit = iota((1, sizes.depth), 1) == cells_ref[0, 2]
                out[at] = out[at] + jnp.where(hit, pulse, 0.0)

            pl.when(inside)(functools.partial(put, c_out, (row, pl.ds(col, 1), slice(None))))
            if last_step:

                @pl.when(core == slot)
                def _():
                    for part, z_out in enumerate(z_outs):
                        here = pl.ds(
                            pl.multiple_of(half * EXTRA + part * sizes.quarter, 16), sizes.quarter
                        )
                        for line in range(sizes.rows):
                            z_out[pl.ds(line * sizes.quarter, sizes.quarter), :] = c_out[
                                line, here, :
                            ]

            else:
                pl.when(inside & (core == slot))(
                    functools.partial(
                        put, z_outs[0], (pl.ds(col + row * sizes.wide, 1), slice(None))
                    )
                )

    operands = (partial, *current, speed, *later)
    if not first_step:
        operands += (gradient,)
    operands += before
    specs = [VMEM] * len(operands) + [SMEM] * 3 + [ANY] * len(settled)
    outs = [(sizes.block, VMEM)] * 2 + [(sizes.pair, VMEM)]
    outs += [(sizes.edges, VMEM)] * 2 if last_step else [(sizes.edge, VMEM)]
    return run(body, f"forward_{step_no}", (*operands, *source, *settled), specs, outs)


def forward_end(sizes, part, partial, beside, speed, later, gradient, settled=()):
    def body(partial_ref, beside_ref, v_ref, later_ref, g_ref, *rest):
        kept_out, sent_out, both = rest[len(settled) :]
        _, half, core = place()
        rows = sizes.rows
        for which in range(2):

            @pl.when(core == which)
            def _():
                @pl.loop(0, sizes.quarter // 8)
                def _(step):
                    local = pl.multiple_of(step * 8, 8)
                    first = pl.multiple_of(half * EXTRA + part * sizes.quarter + local, 8)
                    far = [
                        beside_ref[pl.ds(pl.multiple_of(local + row * sizes.quarter, 8), 8), :]
                        for row in range(rows)
                    ]
                    for slot in range(2):
                        for row in range(rows):
                            at = (slot, row, cut(first), slice(None))
                            total = partial_ref[at]
                            for offset in range(1, REACH + 1):
                                line = row + offset - rows if which else row - offset + rows
                                if slot == which and 0 <= line < rows:
                                    total = total + WEIGHTS[offset] * far[line]
                            total = g_ref[at] + later_ref[at] * total
                            both[slot, row, cut(local), :] = 2.0 * v_ref[at] * total

        kept_out[...] = both[half]
        sent_out[...] = both[1 - half]

    return run(
        body,
        f"forward_end_{part}",
        (partial, beside, speed, later, gradient, *settled),
        [VMEM] * 5 + [ANY] * len(settled),
        [(sizes.quarters, VMEM)] * 2,
        [(2, *sizes.quarters)],
    )


def fill_gradient(sizes, parts, whole=None):
    arrays = [array for _, _, array in parts]
    given = () if whole is None else (whole,)

    def body(*refs):
        out, sems = refs[-2], refs[-1]
        _, half, _ = place()
        copies = Copies(sems)
        for (part, received, _), ref in zip(parts, refs):
            side = 1 - half if received else half
            first = pl.multiple_of(side * sizes.half + part * sizes.quarter, 16)
            copies.start(ref, out.at[:, pl.ds(first, sizes.quarter), :])
        copies.wait()

    return run(
        body,
        f"fill_gradient_{len(given)}",
        (*arrays, *given),
        [ANY] * (len(arrays) + len(given)),
        [(sizes.whole, ANY)],
        aliases={len(arrays): 0} if given else None,
        sems=len(parts),
    )[0]


def fill(sizes, shape, parts, name):
    def body(*refs):
        out, sems = refs[-2], refs[-1]
        _, half, _ = place()
        copies = Copies(sems)
        for index, ref in enumerate(refs[:-2]):
            target = out.at[index // 2, 0] if len(shape) == 5 else out
            side = half if index % 2 == 0 else 1 - half
            if len(ref.shape) == 2:
                ref = ref.at[pl.ds(0, sizes.rows * sizes.half)].reshape(sizes.sent)
            copies.start(ref, target.at[:, sizes.final(side), :])
        copies.wait()

    return run(
        body, name, parts, [ANY] * len(parts), [(shape, ANY)], sems=len(parts)
    )[0]


def on_device(
    wave_state, adjoint_state, velocity, wavelet, traces, source_cells, receiver_cells, start_step
):
    count = lax.axis_size("gx")
    sizes = Sizes(*velocity.shape)
    across = [(i, i ^ 2) for i in range(count)]
    cores = [(i, i ^ 1) for i in range(count)]
    levels = []
    for level in range(count // 4 - 1):
        for half in range(2):
            low, high = 4 * level + 2 * half + 1, 4 * level + 4 + 2 * half
            levels += [(low, high), (high, low)]
    halves = [[i for i in range(count) if (i % 4) // 2 == half] for half in range(2)]

    def over(field):
        return lax.ppermute(field, "gx", across)

    def exchange(block0, block1, edge):
        return (
            block0,
            block1,
            lax.ppermute(block0, "gx", cores),
            lax.ppermute(block1, "gx", cores),
            lax.ppermute(edge, "gx", levels),
        )

    each, steps = traces.shape[2], traces.shape[1]
    sent = pack_first(sizes, velocity, traces[0].T) + pack(sizes, adjoint_state, wave_state)
    velocity_in, later_in, latest_in, current_in, before_in = map(over, sent)
    kept = keep(sizes, velocity, adjoint_state, wave_state)

    speed, tails = speed_begin(sizes, kept[0], velocity_in, sent[0])
    tails = lax.all_gather(tails, "gx", axis_index_groups=halves)
    tails = tails[:, :, :each, :steps].reshape(count // 4, 2, 2, each, steps)
    samples = tails.transpose(4, 0, 2, 1, 3).reshape(1, steps, count * each)
    samples = lax.dynamic_slice_in_dim(samples, start_step[0] + 1, STEPS, 1)

    adjoint = functools.partial(adjoint_step, sizes)
    forward = functools.partial(forward_step, sizes)
    source = (source_cells, wavelet, start_step)

    def ready(step_no, blocks, settled=()):
        return prepare(
            sizes,
            blocks[:4],
            f"prepare_adjoint_{step_no}",
            (step_no, receiver_cells, samples),
            settled,
        )

    def ready_forward(step_no, blocks, settled=()):
        partial = prepare(
            sizes, blocks[:4], f"prepare_forward_{step_no}", settled=settled
        )
        return partial, (*blocks[:2], blocks[4])

    later4, *scaled = adjoint_begin(sizes, speed, kept[1], later_in, samples)
    scaled = exchange(*scaled)
    later3, *scaled = adjoint(
        4, ready(4, scaled), scaled[4], later4, (kept[2], latest_in), speed
    )
    scaled = exchange(*scaled)
    current1 = exchange(*forward_begin(sizes, kept[3], current_in, scaled[:1]))
    later2, *scaled = adjoint(
        3, ready(3, scaled, scaled[4:]), scaled[4], later3, (later4,), speed, current1[:1]
    )
    scaled = exchange(*scaled)
    *current2, image, edge = forward(
        1, *ready_forward(1, current1, (before_in,)), (kept[4], before_in), speed, (), None, source
    )
    current2 = exchange(*current2, edge)
    later1, *scaled, mine1, sent1 = adjoint(
        2, ready(2, scaled), scaled[4], later2, (later3,), speed, current2[:1]
    )
    got1 = over(sent1)
    scaled = exchange(*scaled)
    partial = ready(1, scaled)
    *current3, gradient, edge = forward(
        2,
        *ready_forward(2, current2),
        current1[:2],
        speed,
        (later1, later2),
        image,
        source,
        scaled[2:4],
    )
    current3 = exchange(*current3, edge)
    prepared = ready_forward(3, current3)
    mine0, sent0 = adjoint(1, partial, scaled[4], later1, (later2,), speed, current3[2:4])
    got0 = over(sent0)
    *current4, gradient, edge0, edge1 = forward(
        3, *prepared, current2[:2], speed, (later3,), gradient, source, (mine0, got1)
    )
    *current4, beside0 = exchange(*current4, edge0)
    beside1 = lax.ppermute(edge1, "gx", levels)
    partial, _ = ready_forward(4, (*current4, beside0))
    ends = functools.partial(forward_end, sizes)
    kept0, sent = ends(0, partial, beside0, speed, later4, gradient)
    moved0 = over(sent)
    kept1, sent = ends(1, partial, beside1, speed, later4, gradient, (kept0, got0))
    moved1 = over(sent)
    total = fill_gradient(sizes, [(0, False, kept0), (1, False, kept1), (0, True, moved0)])
    return fill_gradient(sizes, [(1, True, moved1)], total), fill(
        sizes, adjoint_state.shape, [mine0, got0, mine1, got1], "fill_adjoint"
    )


def solution(mesh):
    in_specs = (
        P(None, "groups", "gx", None, None),
        P(None, "groups", "gx", None, None),
        P("gx", "groups", None),
        P("groups", None),
        P("groups", None, "gx"),
        P("groups", None),
        P("groups", None, None),
        P("groups"),
    )
    out_specs = (P("gx", "groups", None), P(None, "groups", "gx", None, None))
    return jax.shard_map(
        on_device, mesh=mesh, in_specs=in_specs, out_specs=out_specs, check_vma=False
    )
```

```python
import functools

import jax
import jax.numpy as jnp
from jax import lax
from jax.experimental import pallas as pl
from jax.experimental.pallas import tpu as pltpu
from jax.sharding import PartitionSpec as P

STEPS = 4
WEIGHTS = (-205.0 / 72.0, 8.0 / 5.0, -1.0 / 5.0, 8.0 / 315.0, -1.0 / 560.0)
UNIT = WEIGHTS[1]
REACH = 4
EXTRA = REACH * STEPS
F32 = jnp.float32
BF16 = jnp.bfloat16
ANY = pl.BlockSpec(memory_space=pl.ANY)
VMEM = pl.BlockSpec(memory_space=pltpu.VMEM)
SMEM = pl.BlockSpec(memory_space=pltpu.SMEM)
MIB = 2**20
PACK_LIMIT = 56


def place():
    position = lax.axis_index("gx")
    return position // 4, (position % 4) // 2, position % 2


def banded(apart):
    band = jnp.zeros(apart.shape, F32)
    for offset in range(1, REACH + 1):
        band = jnp.where(jnp.abs(apart) == offset, WEIGHTS[offset] / UNIT, band)
    return band.astype(BF16)


def iota(shape, axis):
    return lax.broadcasted_iota(jnp.int32, shape, axis)


def two_terms(value):
    high = value.astype(BF16)
    return high, (value - high.astype(F32)).astype(BF16)


def dot(left, right, contract=((1,), (0,))):
    return lax.dot_general(left, right, (contract, ((), ())), preferred_element_type=F32)


class Copies:
    def __init__(self, sems):
        self.sems, self.going = sems, []

    def start(self, source, target):
        copy = pltpu.make_async_copy(source, target, self.sems.at[len(self.going)])
        copy.start()
        self.going.append(copy)

    def wait(self):
        for copy in self.going:
            copy.wait()


class Sizes:
    def __init__(self, rows, cols, depth):
        self.rows, self.cols, self.depth = rows, cols, depth
        self.half = cols // 2
        self.wide = self.half + EXTRA
        self.pair = (2, rows, self.wide, depth)
        self.block = (rows, self.wide, depth)
        self.edge = (rows * self.wide + 8, depth)
        self.moved = (rows * self.wide + 16, depth)
        self.sent = (rows, self.half, depth)
        self.whole = (rows, cols, depth)
        self.back = (rows * self.half + 8, depth)
        self.quarter = cols // 4
        self.quarters = (rows, self.quarter, depth)
        self.edges = (rows * self.quarter, depth)

    def window(self, half):
        return pl.ds(pl.multiple_of(half * (self.half - EXTRA), 16), self.wide)

    def own(self, half):
        return pl.ds(pl.multiple_of(half * EXTRA, 16), self.half)

    def final(self, half):
        return pl.ds(pl.multiple_of(half * self.half, 16), self.half)

    def moved_row(self, row):
        return pl.ds(row * self.wide, self.wide)

    @property
    def moved_tail(self):
        return pl.ds(self.rows * self.wide, 16)


def over_columns(count, body):
    @pl.loop(0, count // 16)
    def _(step):
        for part in range(2):
            body(pl.multiple_of(step * 16 + part * 8, 8))


def cut(first):
    return pl.ds(first, 8)


def flat(sizes, row, first):
    return pl.ds(pl.multiple_of(first + row * sizes.wide, 8), 8), slice(None)


def merged(sizes, own, moved, slot, row, first):
    _, half, _ = place()
    received = moved[flat(sizes, row, first)]
    return jnp.where(half == slot, own[row, cut(first), :], received)


def differences(sizes, blocks, mixed, added=None):
    wide, depth = sizes.wide, sizes.depth
    shape = (wide, 2 * wide)
    column = iota(shape, 1)
    column = jnp.where(column >= wide, column - wide, column)
    band_y = banded(iota(shape, 0) - column)
    shape = (2 * depth, depth)
    layer = iota(shape, 0)
    layer = jnp.where(layer >= depth, layer - depth, layer)
    band_z = banded(layer - iota(shape, 1))
    for slot in range(2):
        for row in range(sizes.rows):
            terms = two_terms(blocks[slot][row])
            total = dot(jnp.concatenate(terms, 1), band_z)
            total = UNIT * (total + dot(band_y, jnp.concatenate(terms, 0)))
            if added is not None:
                total = total + added(slot, row)
            mixed[slot, row] = total


def along_rows(sizes, blocks, mixed, partial, narrow=False):
    mine0, mine1, other0, other1 = blocks
    rows = sizes.rows
    _, half, core = place()
    orders = (
        (None, mine0, other0, mine1, other1),
        (other0, mine0, other1, mine1, None),
    )
    for which, order in enumerate(orders):

        @pl.when(core == which)
        def _():
            for slot in range(2):

                def columns(local):
                    first = local
                    if narrow:
                        first = pl.multiple_of(half * EXTRA + local, 8)
                    near = [
                        None
                        if block is None
                        else block[
                            row, cut(first if block is mine0 or block is mine1 else local), :
                        ]
                        for block in order[2 * slot : 2 * slot + 3]
                        for row in range(rows)
                    ]
                    for row in range(rows):
                        parts = []
                        for offset in range(1, REACH + 1):
                            pair = (near[rows + row + offset], near[rows + row - offset])
                            pair = [value for value in pair if value is not None]
                            if pair:
                                parts.append(WEIGHTS[offset] * sum(pair[1:], pair[0]))
                        total = 3.0 * WEIGHTS[0] * near[rows + row]
                        total = total + mixed[slot, row, cut(first), :]
                        partial[slot, row, cut(first), :] = sum(parts[1:], parts[0]) + total

                over_columns(sizes.half if narrow else sizes.wide, columns)


def prepare(sizes, blocks, name, inject=None, settled=(), narrow=False):
    def body(*refs):
        b_refs = refs[:4]
        partial, mixed = refs[-2:]
        added = None
        if inject is not None:
            step_no = inject[0]
            cells_ref, samples_ref = refs[4:6]
            level, half, core = place()
            where_x, where_y, where_z = (cells_ref[0, axis : axis + 1, :] for axis in range(3))
            count = where_x.shape[1]
            values = jnp.where(
                where_z == iota((sizes.depth, count), 0),
                samples_ref[0, step_no - 1 : step_no, :],
                0.0,
            )
            values = jnp.concatenate(two_terms(values), 1)
            col_ids = iota((sizes.wide, count), 0) + half * (sizes.half - EXTRA)

            def added(slot, row):
                this_row = ((level * 2 + slot) * 2 + core) * sizes.rows + row
                col_of = jnp.where(where_x == this_row, where_y, -1)
                hit = jnp.where(col_of == col_ids, 1.0, 0.0).astype(BF16)
                return dot(jnp.concatenate((hit, hit), 1), values, ((1,), (1,)))

        differences(sizes, b_refs, mixed, added)
        along_rows(sizes, b_refs, mixed, partial, narrow)

    operands = (*blocks, *(inject[1:] if inject is not None else ()))
    specs = [VMEM] * len(operands) + [ANY] * len(settled)
    return run(
        body,
        name,
        (*operands, *settled),
        specs,
        [(sizes.pair, VMEM)],
        [sizes.pair],
    )[0]


def sweep(sizes, partial, beside, finish):
    rows = sizes.rows
    _, _, core = place()
    for which in range(2):

        @pl.when(core == which)
        def _():
            def columns(first):
                far = [beside[flat(sizes, row, first)] for row in range(rows)]
                for slot in range(2):
                    for row in range(rows):
                        total = partial[slot, row, cut(first), :]
                        for offset in range(1, REACH + 1):
                            at = row + offset - rows if which else row - offset + rows
                            if slot == which and 0 <= at < rows:
                                total = total + WEIGHTS[offset] * far[at]
                        finish(which, slot, row, first, total)

            over_columns(sizes.wide, columns)


def run(body, name, operands, specs, outs, scratch=(), aliases=None, limit=24, sems=0):
    return pl.pallas_call(
        body,
        name=name,
        out_shape=[jax.ShapeDtypeStruct(shape, F32) for shape, _ in outs],
        in_specs=specs,
        out_specs=[spec for _, spec in outs],
        scratch_shapes=[pltpu.VMEM(shape, F32) for shape in scratch]
        + ([pltpu.SemaphoreType.DMA((sems,))] if sems else []),
        input_output_aliases=aliases or {},
        compiler_params=pltpu.CompilerParams(vmem_limit_bytes=limit * MIB),
        cost_estimate=pl.CostEstimate(flops=0, bytes_accessed=0, transcendentals=0),
    )(*operands)


def pack_first(sizes, velocity, traces):
    def body(field, traces_ref, out, sems):
        _, half, _ = place()
        copies = Copies(sems)
        copies.start(
            field.at[:, sizes.window(1 - half), :],
            out.at[pl.ds(0, sizes.rows * sizes.wide)].reshape(sizes.block),
        )
        each, steps = traces_ref.shape
        out[sizes.moved_tail, :] = jnp.zeros((16, sizes.depth), F32)
        out[pl.ds(sizes.rows * sizes.wide, each), :steps] = traces_ref[...]
        copies.wait()

    return run(
        body,
        "pack_first",
        (velocity, traces),
        [ANY, VMEM],
        [(sizes.moved, VMEM)],
        limit=16,
        sems=1,
    )


def pack(sizes, adjoint, wave):
    def body(a_ref, w_ref, *rest):
        outs, sems = rest[:4], rest[4]
        _, half, _ = place()
        copies = Copies(sems)
        fields = (a_ref.at[0, 0], a_ref.at[1, 0], w_ref.at[1, 0], w_ref.at[0, 0])
        for field, out in zip(fields, outs):
            copies.start(
                field.at[:, sizes.window(1 - half), :],
                out.at[pl.ds(0, sizes.rows * sizes.wide)].reshape(sizes.block),
            )
            out[sizes.moved_tail, :] = jnp.zeros((16, sizes.depth), F32)
        copies.wait()

    return run(
        body,
        "pack",
        (adjoint, wave),
        [ANY] * 2,
        [(sizes.moved, VMEM)] * 4,
        limit=PACK_LIMIT,
        sems=4,
    )


def keep(sizes, velocity, adjoint, wave):
    def body(v_ref, a_ref, w_ref, *rest):
        outs, sems = rest[:5], rest[5]
        _, half, _ = place()
        copies = Copies(sems)
        fields = (v_ref, a_ref.at[0, 0], a_ref.at[1, 0], w_ref.at[1, 0], w_ref.at[0, 0])
        for field, out in zip(fields, outs):
            copies.start(field.at[:, sizes.window(half), :], out)
        copies.wait()

    return run(
        body,
        "keep",
        (velocity, adjoint, wave),
        [ANY] * 3,
        [(sizes.block, VMEM)] * 5,
        limit=PACK_LIMIT,
        sems=5,
    )


def speed_begin(sizes, own, moved, sent):
    def body(own_ref, moved_ref, sent_ref, v_out, tail_out):
        _, half, _ = place()
        tail_out[half] = sent_ref[sizes.moved_tail, :]
        tail_out[1 - half] = moved_ref[sizes.moved_tail, :]

        def columns(first):
            for slot in range(2):
                for row in range(sizes.rows):
                    v_out[slot, row, cut(first), :] = merged(
                        sizes, own_ref, moved_ref, slot, row, first
                    )

        over_columns(sizes.wide, columns)

    return run(
        body,
        "speed_begin",
        (own, moved, sent),
        [VMEM] * 3,
        [(sizes.pair, VMEM), ((2, 16, sizes.depth), VMEM)],
    )


def adjoint_begin(sizes, speed, own, moved, settled):
    def body(v_ref, own_ref, moved_ref, _, a_out, u0_out, u1_out, z_out):
        _, _, core = place()

        def columns(first):
            for slot, u_out in enumerate((u0_out, u1_out)):
                for row in range(sizes.rows):
                    value = merged(sizes, own_ref, moved_ref, slot, row, first)
                    a_out[slot, row, cut(first), :] = value
                    here = v_ref[slot, row, cut(first), :]
                    u_out[row, cut(first), :] = here * here * value
            for row in range(sizes.rows):
                z_out[flat(sizes, row, first)] = jnp.where(
                    core == 0, u0_out[row, cut(first), :], u1_out[row, cut(first), :]
                )

        over_columns(sizes.wide, columns)

    return run(
        body,
        "adjoint_begin",
        (speed, own, moved, settled),
        [VMEM] * 3 + [ANY],
        [(sizes.pair, VMEM)] + [(sizes.block, VMEM)] * 2 + [(sizes.edge, VMEM)],
    )


def adjoint_step(sizes, step_no, partial, beside, later, latest, speed, settled=()):
    split = len(latest) == 2
    more = step_no > 1
    ends = step_no <= 2

    def body(*refs):
        refs = list(refs)
        partial_ref, beside_ref, later_ref, v_ref = refs[:4]
        latest_refs, refs = refs[4 : 4 + len(latest)], refs[4 + len(latest) + len(settled) :]
        if more:
            (next_out, u0_out, u1_out, z_out), refs = refs[:4], refs[4:]
        if ends:
            (kept_out, sent_out), refs = refs[:2], refs[2:]
        if not more:
            next_out = refs.pop(0)
        _, half, _ = place()

        def finish(which, slot, row, first, total):
            at = (slot, row, cut(first), slice(None))
            if split:
                last = merged(sizes, *latest_refs, slot, row, first)
            else:
                last = latest_refs[0][at]
            value = 2.0 * later_ref[at] - last + total
            next_out[at] = value
            if more:
                here = v_ref[at]
                value = here * here * value
                (u0_out, u1_out)[slot][row, cut(first), :] = value
                if which == slot:
                    z_out[flat(sizes, row, first)] = value

        sweep(sizes, partial_ref, beside_ref, finish)
        if ends:
            kept_out[...] = next_out[half, :, sizes.own(half), :]
            for row in range(sizes.rows):
                sent_out[pl.ds(row * sizes.half, sizes.half), :] = next_out[
                    1 - half, row, sizes.own(half), :
                ]
            rest = sent_out.shape[0] - sizes.rows * sizes.half
            sent_out[pl.ds(sizes.rows * sizes.half, rest), :] = jnp.zeros((rest, sizes.depth), F32)

    outs = []
    if more:
        outs += [(sizes.pair, VMEM)] + [(sizes.block, VMEM)] * 2 + [(sizes.edge, VMEM)]
    if ends:
        outs += [(sizes.sent, VMEM), (sizes.moved if more else sizes.back, VMEM)]
    return run(
        body,
        f"adjoint_{step_no}",
        (partial, beside, later, speed, *latest, *settled),
        [VMEM] * (4 + len(latest)) + [ANY] * len(settled),
        outs,
        [] if more else [sizes.pair],
    )


def forward_begin(sizes, own, moved, settled):
    def body(own_ref, moved_ref, *rest):
        c0_out, c1_out, z_out = rest[len(settled) :]
        _, _, core = place()

        def columns(first):
            for row in range(sizes.rows):
                pair = [merged(sizes, own_ref, moved_ref, slot, row, first) for slot in range(2)]
                c0_out[row, cut(first), :] = pair[0]
                c1_out[row, cut(first), :] = pair[1]
                z_out[flat(sizes, row, first)] = jnp.where(core == 0, *pair)

        over_columns(sizes.wide, columns)

    return run(
        body,
        "forward_begin",
        (own, moved, *settled),
        [VMEM] * 2 + [ANY] * len(settled),
        [(sizes.block, VMEM)] * 2 + [(sizes.edge, VMEM)],
    )


def forward_step(
    sizes, step_no, partial, current, before, speed, later, gradient, source, settled=()
):
    first_step = step_no == 1
    last_step = step_no == STEPS - 1

    def body(*refs):
        refs = list(refs)
        partial_ref, c_refs, beside_ref, v_ref, refs = refs[0], refs[1:3], refs[3], refs[4], refs[5:]
        late, refs = refs[: len(later)], refs[len(later) :]
        if not first_step:
            g_ref, refs = refs[0], refs[1:]
        before_refs, refs = refs[:2], refs[2:]
        (cells_ref, wavelet_ref, start_ref), refs = refs[:3], refs[3:]
        c0_out, c1_out, g_out, *z_outs = refs[len(settled) :]
        level, half, core = place()

        def finish(which, slot, row, first, total):
            at = (slot, row, cut(first), slice(None))
            if first_step:
                g_out[at] = total
            elif step_no == 2:
                g_out[at] = late[0][at] * g_ref[at] + late[1][at] * total
            else:
                g_out[at] = g_ref[at] + late[0][at] * total
            if first_step:
                last = merged(sizes, *before_refs, slot, row, first)
            else:
                last = before_refs[slot][row, cut(first), :]
            here = v_ref[at]
            centre = c_refs[slot][row, cut(first), :]
            value = 2.0 * centre - last + here * here * total
            (c0_out, c1_out)[slot][row, cut(first), :] = value
            if which == slot and not last_step:
                z_outs[0][flat(sizes, row, first)] = value

        sweep(sizes, partial_ref, beside_ref, finish)
        col = cells_ref[0, 1] - half * (sizes.half - EXTRA)
        pulse = wavelet_ref[0, start_ref[0] + step_no]
        for slot, c_out in enumerate((c0_out, c1_out)):
            row = cells_ref[0, 0] - ((level * 2 + slot) * 2 + core) * sizes.rows
            inside = (row >= 0) & (row < sizes.rows) & (col >= 0) & (col < sizes.wide)

            def put(out, at):
                hit = iota((1, sizes.depth), 1) == cells_ref[0, 2]
                out[at] = out[at] + jnp.where(hit, pulse, 0.0)

            pl.when(inside)(functools.partial(put, c_out, (row, pl.ds(col, 1), slice(None))))
            if last_step:

                z_outs[slot][...] = c_out[:, sizes.own(half), :]

                @pl.when(core == slot)
                def _():
                    for part, z_out in enumerate(z_outs[2:]):
                        here = pl.ds(
                            pl.multiple_of(half * EXTRA + part * sizes.quarter, 16), sizes.quarter
                        )
                        for line in range(sizes.rows):
                            z_out[pl.ds(line * sizes.quarter, sizes.quarter), :] = c_out[
                                line, here, :
                            ]

            else:
                pl.when(inside & (core == slot))(
                    functools.partial(
                        put, z_outs[0], (pl.ds(col + row * sizes.wide, 1), slice(None))
                    )
                )

    operands = (partial, *current, speed, *later)
    if not first_step:
        operands += (gradient,)
    operands += before
    specs = [VMEM] * len(operands) + [SMEM] * 3 + [ANY] * len(settled)
    outs = [(sizes.block, VMEM)] * 2 + [(sizes.pair, VMEM)]
    if last_step:
        outs += [(sizes.sent, VMEM)] * 2 + [(sizes.edges, VMEM)] * 2
    else:
        outs += [(sizes.edge, VMEM)]
    return run(body, f"forward_{step_no}", (*operands, *source, *settled), specs, outs)


def forward_end(sizes, part, partial, beside, speed, later, gradient, settled=()):
    def body(partial_ref, beside_ref, v_ref, later_ref, g_ref, *rest):
        kept_out, sent_out, both = rest[len(settled) :]
        _, half, core = place()
        rows = sizes.rows
        for which in range(2):

            @pl.when(core == which)
            def _():
                @pl.loop(0, sizes.quarter // 8)
                def _(step):
                    local = pl.multiple_of(step * 8, 8)
                    first = pl.multiple_of(half * EXTRA + part * sizes.quarter + local, 8)
                    far = [
                        beside_ref[pl.ds(pl.multiple_of(local + row * sizes.quarter, 8), 8), :]
                        for row in range(rows)
                    ]
                    for slot in range(2):
                        for row in range(rows):
                            at = (slot, row, cut(first), slice(None))
                            total = partial_ref[at]
                            for offset in range(1, REACH + 1):
                                line = row + offset - rows if which else row - offset + rows
                                if slot == which and 0 <= line < rows:
                                    total = total + WEIGHTS[offset] * far[line]
                            total = g_ref[at] + later_ref[at] * total
                            both[slot, row, cut(local), :] = 2.0 * v_ref[at] * total

        kept_out[...] = both[half]
        sent_out[...] = both[1 - half]

    return run(
        body,
        f"forward_end_{part}",
        (partial, beside, speed, later, gradient, *settled),
        [VMEM] * 5 + [ANY] * len(settled),
        [(sizes.quarters, VMEM)] * 2,
        [(2, *sizes.quarters)],
    )


def fill_gradient(sizes, parts, whole=None):
    arrays = [array for _, _, array in parts]
    given = () if whole is None else (whole,)

    def body(*refs):
        out, sems = refs[-2], refs[-1]
        _, half, _ = place()
        copies = Copies(sems)
        for (part, received, _), ref in zip(parts, refs):
            side = 1 - half if received else half
            first = pl.multiple_of(side * sizes.half + part * sizes.quarter, 16)
            copies.start(ref, out.at[:, pl.ds(first, sizes.quarter), :])
        copies.wait()

    return run(
        body,
        f"fill_gradient_{len(given)}",
        (*arrays, *given),
        [ANY] * (len(arrays) + len(given)),
        [(sizes.whole, ANY)],
        aliases={len(arrays): 0} if given else None,
        sems=len(parts),
    )[0]


def fill(sizes, shape, parts, name):
    def body(*refs):
        out, sems = refs[-2], refs[-1]
        _, half, _ = place()
        copies = Copies(sems)
        for index, ref in enumerate(refs[:-2]):
            target = out.at[index // 2, 0] if len(shape) == 5 else out
            side = half if index % 2 == 0 else 1 - half
            if len(ref.shape) == 2:
                ref = ref.at[pl.ds(0, sizes.rows * sizes.half)].reshape(sizes.sent)
            copies.start(ref, target.at[:, sizes.final(side), :])
        copies.wait()

    return run(
        body, name, parts, [ANY] * len(parts), [(shape, ANY)], sems=len(parts)
    )[0]


def on_device(
    wave_state, adjoint_state, velocity, wavelet, traces, source_cells, receiver_cells, start_step
):
    count = lax.axis_size("gx")
    sizes = Sizes(*velocity.shape)
    across = [(i, i ^ 2) for i in range(count)]
    cores = [(i, i ^ 1) for i in range(count)]
    levels = []
    for level in range(count // 4 - 1):
        for half in range(2):
            low, high = 4 * level + 2 * half + 1, 4 * level + 4 + 2 * half
            levels += [(low, high), (high, low)]
    halves = [[i for i in range(count) if (i % 4) // 2 == half] for half in range(2)]

    def over(field):
        return lax.ppermute(field, "gx", across)

    def exchange(block0, block1, edge):
        return (
            block0,
            block1,
            lax.ppermute(block0, "gx", cores),
            lax.ppermute(block1, "gx", cores),
            lax.ppermute(edge, "gx", levels),
        )

    each, steps = traces.shape[2], traces.shape[1]
    sent = pack_first(sizes, velocity, traces[0].T) + pack(sizes, adjoint_state, wave_state)
    velocity_in, later_in, latest_in, current_in, before_in = map(over, sent)
    kept = keep(sizes, velocity, adjoint_state, wave_state)

    speed, tails = speed_begin(sizes, kept[0], velocity_in, sent[0])
    tails = lax.all_gather(tails, "gx", axis_index_groups=halves)
    tails = tails[:, :, :each, :steps].reshape(count // 4, 2, 2, each, steps)
    samples = tails.transpose(4, 0, 2, 1, 3).reshape(1, steps, count * each)
    samples = lax.dynamic_slice_in_dim(samples, start_step[0] + 1, STEPS, 1)

    adjoint = functools.partial(adjoint_step, sizes)
    forward = functools.partial(forward_step, sizes)
    source = (source_cells, wavelet, start_step)

    def ready(step_no, blocks, settled=()):
        return prepare(
            sizes,
            blocks[:4],
            f"prepare_adjoint_{step_no}",
            (step_no, receiver_cells, samples),
            settled,
        )

    def ready_forward(step_no, blocks, settled=()):
        partial = prepare(
            sizes, blocks[:4], f"prepare_forward_{step_no}", settled=settled
        )
        return partial, (*blocks[:2], blocks[4])

    later4, *scaled = adjoint_begin(sizes, speed, kept[1], later_in, samples)
    scaled = exchange(*scaled)
    later3, *scaled = adjoint(
        4, ready(4, scaled), scaled[4], later4, (kept[2], latest_in), speed
    )
    scaled = exchange(*scaled)
    current1 = exchange(*forward_begin(sizes, kept[3], current_in, scaled[:1]))
    later2, *scaled = adjoint(
        3, ready(3, scaled, scaled[4:]), scaled[4], later3, (later4,), speed, current1[:1]
    )
    scaled = exchange(*scaled)
    *current2, image, edge = forward(
        1, *ready_forward(1, current1, (before_in,)), (kept[4], before_in), speed, (), None, source
    )
    current2 = exchange(*current2, edge)
    later1, *scaled, mine1, sent1 = adjoint(
        2, ready(2, scaled), scaled[4], later2, (later3,), speed, current2[:1]
    )
    got1 = over(sent1)
    scaled = exchange(*scaled)
    partial = ready(1, scaled)
    *current3, gradient, edge = forward(
        2,
        *ready_forward(2, current2),
        current1[:2],
        speed,
        (later1, later2),
        image,
        source,
        scaled[2:4],
    )
    current3 = exchange(*current3, edge)
    prepared = ready_forward(3, current3)
    mine0, sent0 = adjoint(1, partial, scaled[4], later1, (later2,), speed, current3[2:4])
    got0 = over(sent0)
    *current4, gradient, narrow0, narrow1, edge0, edge1 = forward(
        3, *prepared, current2[:2], speed, (later3,), gradient, source, (mine0, got1)
    )
    *narrow4, beside0 = exchange(narrow0, narrow1, edge0)[2:]
    beside1 = lax.ppermute(edge1, "gx", levels)
    partial = prepare(sizes, (*current4, *narrow4), "prepare_forward_4", narrow=True)
    ends = functools.partial(forward_end, sizes)
    kept0, sent = ends(0, partial, beside0, speed, later4, gradient)
    moved0 = over(sent)
    kept1, sent = ends(1, partial, beside1, speed, later4, gradient, (kept0, got0))
    moved1 = over(sent)
    total = fill_gradient(sizes, [(0, False, kept0), (1, False, kept1), (0, True, moved0)])
    return fill_gradient(sizes, [(1, True, moved1)], total), fill(
        sizes, adjoint_state.shape, [mine0, got0, mine1, got1], "fill_adjoint"
    )


def solution(mesh):
    in_specs = (
        P(None, "groups", "gx", None, None),
        P(None, "groups", "gx", None, None),
        P("gx", "groups", None),
        P("groups", None),
        P("groups", None, "gx"),
        P("groups", None),
        P("groups", None, None),
        P("groups"),
    )
    out_specs = (P("gx", "groups", None), P(None, "groups", "gx", None, None))
    return jax.shard_map(
        on_device, mesh=mesh, in_specs=in_specs, out_specs=out_specs, check_vma=False
    )
```

```python
import functools

import jax
import jax.numpy as jnp
from jax import lax
from jax.experimental import pallas as pl
from jax.experimental.pallas import tpu as pltpu
from jax.sharding import PartitionSpec as P

STEPS = 4
WEIGHTS = (-205.0 / 72.0, 8.0 / 5.0, -1.0 / 5.0, 8.0 / 315.0, -1.0 / 560.0)
UNIT = WEIGHTS[1]
REACH = 4
EXTRA = REACH * STEPS
F32 = jnp.float32
BF16 = jnp.bfloat16
ANY = pl.BlockSpec(memory_space=pl.ANY)
VMEM = pl.BlockSpec(memory_space=pltpu.VMEM)
SMEM = pl.BlockSpec(memory_space=pltpu.SMEM)
MIB = 2**20
PACK_LIMIT = 56


def place():
    position = lax.axis_index("gx")
    return position // 4, (position % 4) // 2, position % 2


def banded(apart):
    band = jnp.zeros(apart.shape, F32)
    for offset in range(1, REACH + 1):
        band = jnp.where(jnp.abs(apart) == offset, WEIGHTS[offset] / UNIT, band)
    return band.astype(BF16)


def iota(shape, axis):
    return lax.broadcasted_iota(jnp.int32, shape, axis)


def two_terms(value):
    high = value.astype(BF16)
    return high, (value - high.astype(F32)).astype(BF16)


def dot(left, right, contract=((1,), (0,))):
    return lax.dot_general(left, right, (contract, ((), ())), preferred_element_type=F32)


class Copies:
    def __init__(self, sems):
        self.sems, self.going = sems, []

    def start(self, source, target):
        copy = pltpu.make_async_copy(source, target, self.sems.at[len(self.going)])
        copy.start()
        self.going.append(copy)

    def wait(self):
        for copy in self.going:
            copy.wait()


class Sizes:
    def __init__(self, rows, cols, depth):
        self.rows, self.cols, self.depth = rows, cols, depth
        self.half = cols // 2
        self.wide = self.half + EXTRA
        self.pair = (2, rows, self.wide, depth)
        self.block = (rows, self.wide, depth)
        self.edge = (rows * self.wide + 8, depth)
        self.moved = (rows * self.wide + 16, depth)
        self.sent = (rows, self.half, depth)
        self.whole = (rows, cols, depth)
        self.back = (rows * self.half + 8, depth)
        self.quarter = cols // 4
        self.quarters = (rows, self.quarter, depth)
        self.edges = (rows * self.quarter, depth)

    def window(self, half):
        return pl.ds(pl.multiple_of(half * (self.half - EXTRA), 16), self.wide)

    def own(self, half):
        return pl.ds(pl.multiple_of(half * EXTRA, 16), self.half)

    def final(self, half):
        return pl.ds(pl.multiple_of(half * self.half, 16), self.half)

    def moved_row(self, row):
        return pl.ds(row * self.wide, self.wide)

    @property
    def moved_tail(self):
        return pl.ds(self.rows * self.wide, 16)


def over_columns(count, body):
    @pl.loop(0, count // 16)
    def _(step):
        for part in range(2):
            body(pl.multiple_of(step * 16 + part * 8, 8))


def cut(first):
    return pl.ds(first, 8)


def flat(sizes, row, first):
    return pl.ds(pl.multiple_of(first + row * sizes.wide, 8), 8), slice(None)


def merged(sizes, own, moved, slot, row, first):
    _, half, _ = place()
    received = moved[flat(sizes, row, first)]
    return jnp.where(half == slot, own[row, cut(first), :], received)


def differences(sizes, blocks, mixed, added=None):
    wide, depth = sizes.wide, sizes.depth
    shape = (wide, 2 * wide)
    column = iota(shape, 1)
    column = jnp.where(column >= wide, column - wide, column)
    band_y = banded(iota(shape, 0) - column)
    shape = (2 * depth, depth)
    layer = iota(shape, 0)
    layer = jnp.where(layer >= depth, layer - depth, layer)
    band_z = banded(layer - iota(shape, 1))
    for slot in range(2):
        for row in range(sizes.rows):
            terms = two_terms(blocks[slot][row])
            total = dot(jnp.concatenate(terms, 1), band_z)
            total = UNIT * (total + dot(band_y, jnp.concatenate(terms, 0)))
            if added is not None:
                total = total + added(slot, row)
            mixed[slot, row] = total


def along_rows(sizes, blocks, mixed, partial, narrow=False):
    mine0, mine1, other0, other1 = blocks
    rows = sizes.rows
    _, half, core = place()
    orders = (
        (None, mine0, other0, mine1, other1),
        (other0, mine0, other1, mine1, None),
    )
    for which, order in enumerate(orders):

        @pl.when(core == which)
        def _():
            for slot in range(2):

                def columns(local):
                    first = local
                    if narrow:
                        first = pl.multiple_of(half * EXTRA + local, 8)
                    near = [
                        None
                        if block is None
                        else block[
                            row, cut(first if block is mine0 or block is mine1 else local), :
                        ]
                        for block in order[2 * slot : 2 * slot + 3]
                        for row in range(rows)
                    ]
                    for row in range(rows):
                        parts = []
                        for offset in range(1, REACH + 1):
                            pair = (near[rows + row + offset], near[rows + row - offset])
                            pair = [value for value in pair if value is not None]
                            if pair:
                                parts.append(WEIGHTS[offset] * sum(pair[1:], pair[0]))
                        total = 3.0 * WEIGHTS[0] * near[rows + row]
                        total = total + mixed[slot, row, cut(first), :]
                        partial[slot, row, cut(first), :] = sum(parts[1:], parts[0]) + total

                over_columns(sizes.half if narrow else sizes.wide, columns)


def prepare(sizes, blocks, name, inject=None, settled=(), narrow=False):
    def body(*refs):
        b_refs = refs[:4]
        partial, mixed = refs[-2:]
        added = None
        if inject is not None:
            step_no = inject[0]
            cells_ref, samples_ref = refs[4:6]
            level, half, core = place()
            where_x, where_y, where_z = (cells_ref[0, axis : axis + 1, :] for axis in range(3))
            count = where_x.shape[1]
            values = jnp.where(
                where_z == iota((sizes.depth, count), 0),
                samples_ref[0, step_no - 1 : step_no, :],
                0.0,
            )
            values = jnp.concatenate(two_terms(values), 1)
            col_ids = iota((sizes.wide, count), 0) + half * (sizes.half - EXTRA)

            def added(slot, row):
                this_row = ((level * 2 + slot) * 2 + core) * sizes.rows + row
                col_of = jnp.where(where_x == this_row, where_y, -1)
                hit = jnp.where(col_of == col_ids, 1.0, 0.0).astype(BF16)
                return dot(jnp.concatenate((hit, hit), 1), values, ((1,), (1,)))

        differences(sizes, b_refs, mixed, added)
        along_rows(sizes, b_refs, mixed, partial, narrow)

    operands = (*blocks, *(inject[1:] if inject is not None else ()))
    specs = [VMEM] * len(operands) + [ANY] * len(settled)
    return run(
        body,
        name,
        (*operands, *settled),
        specs,
        [(sizes.pair, VMEM)],
        [sizes.pair],
    )[0]


def sweep(sizes, partial, beside, finish):
    rows = sizes.rows
    _, _, core = place()
    for which in range(2):

        @pl.when(core == which)
        def _():
            def columns(first):
                far = [beside[flat(sizes, row, first)] for row in range(rows)]
                for slot in range(2):
                    for row in range(rows):
                        total = partial[slot, row, cut(first), :]
                        for offset in range(1, REACH + 1):
                            at = row + offset - rows if which else row - offset + rows
                            if slot == which and 0 <= at < rows:
                                total = total + WEIGHTS[offset] * far[at]
                        finish(which, slot, row, first, total)

            over_columns(sizes.wide, columns)


def run(body, name, operands, specs, outs, scratch=(), aliases=None, limit=24, sems=0):
    return pl.pallas_call(
        body,
        name=name,
        out_shape=[jax.ShapeDtypeStruct(shape, F32) for shape, _ in outs],
        in_specs=specs,
        out_specs=[spec for _, spec in outs],
        scratch_shapes=[pltpu.VMEM(shape, F32) for shape in scratch]
        + ([pltpu.SemaphoreType.DMA((sems,))] if sems else []),
        input_output_aliases=aliases or {},
        compiler_params=pltpu.CompilerParams(vmem_limit_bytes=limit * MIB),
        cost_estimate=pl.CostEstimate(flops=0, bytes_accessed=0, transcendentals=0),
    )(*operands)


def pack_first(sizes, velocity, traces):
    def body(field, traces_ref, out, sems):
        _, half, _ = place()
        copies = Copies(sems)
        copies.start(
            field.at[:, sizes.window(1 - half), :],
            out.at[pl.ds(0, sizes.rows * sizes.wide)].reshape(sizes.block),
        )
        each, steps = traces_ref.shape
        out[sizes.moved_tail, :] = jnp.zeros((16, sizes.depth), F32)
        out[pl.ds(sizes.rows * sizes.wide, each), :steps] = traces_ref[...]
        copies.wait()

    return run(
        body,
        "pack_first",
        (velocity, traces),
        [ANY, VMEM],
        [(sizes.moved, VMEM)],
        limit=16,
        sems=1,
    )


def pack(sizes, adjoint, wave):
    def body(a_ref, w_ref, *rest):
        outs, sems = rest[:4], rest[4]
        _, half, _ = place()
        copies = Copies(sems)
        fields = (a_ref.at[0, 0], a_ref.at[1, 0], w_ref.at[1, 0], w_ref.at[0, 0])
        for field, out in zip(fields, outs):
            copies.start(
                field.at[:, sizes.window(1 - half), :],
                out.at[pl.ds(0, sizes.rows * sizes.wide)].reshape(sizes.block),
            )
            tail = pl.ds(sizes.rows * sizes.wide, 8)
            out[tail, :] = jnp.zeros((8, sizes.depth), F32)
        copies.wait()

    return run(
        body,
        "pack",
        (adjoint, wave),
        [ANY] * 2,
        [(sizes.edge, VMEM)] * 4,
        limit=PACK_LIMIT,
        sems=4,
    )


def keep(sizes, velocity, adjoint, wave):
    def body(v_ref, a_ref, w_ref, *rest):
        outs, sems = rest[:5], rest[5]
        _, half, _ = place()
        copies = Copies(sems)
        fields = (v_ref, a_ref.at[0, 0], a_ref.at[1, 0], w_ref.at[1, 0], w_ref.at[0, 0])
        for field, out in zip(fields, outs):
            copies.start(field.at[:, sizes.window(half), :], out)
        copies.wait()

    return run(
        body,
        "keep",
        (velocity, adjoint, wave),
        [ANY] * 3,
        [(sizes.block, VMEM)] * 5,
        limit=PACK_LIMIT,
        sems=5,
    )


def speed_begin(sizes, own, moved, sent):
    def body(own_ref, moved_ref, sent_ref, v_out, tail_out):
        _, half, _ = place()
        tail_out[half] = sent_ref[sizes.moved_tail, :]
        tail_out[1 - half] = moved_ref[sizes.moved_tail, :]

        def columns(first):
            for slot in range(2):
                for row in range(sizes.rows):
                    v_out[slot, row, cut(first), :] = merged(
                        sizes, own_ref, moved_ref, slot, row, first
                    )

        over_columns(sizes.wide, columns)

    return run(
        body,
        "speed_begin",
        (own, moved, sent),
        [VMEM] * 3,
        [(sizes.pair, VMEM), ((2, 16, sizes.depth), VMEM)],
    )


def adjoint_begin(sizes, speed, own, moved, settled):
    def body(v_ref, own_ref, moved_ref, _, a_out, u0_out, u1_out, z_out):
        _, _, core = place()

        def columns(first):
            for slot, u_out in enumerate((u0_out, u1_out)):
                for row in range(sizes.rows):
                    value = merged(sizes, own_ref, moved_ref, slot, row, first)
                    a_out[slot, row, cut(first), :] = value
                    here = v_ref[slot, row, cut(first), :]
                    u_out[row, cut(first), :] = here * here * value
            for row in range(sizes.rows):
                z_out[flat(sizes, row, first)] = jnp.where(
                    core == 0, u0_out[row, cut(first), :], u1_out[row, cut(first), :]
                )

        over_columns(sizes.wide, columns)

    return run(
        body,
        "adjoint_begin",
        (speed, own, moved, settled),
        [VMEM] * 3 + [ANY],
        [(sizes.pair, VMEM)] + [(sizes.block, VMEM)] * 2 + [(sizes.edge, VMEM)],
    )


def adjoint_step(sizes, step_no, partial, beside, later, latest, speed, settled=()):
    split = len(latest) == 2
    more = step_no > 1
    ends = step_no <= 2

    def body(*refs):
        refs = list(refs)
        partial_ref, beside_ref, later_ref, v_ref = refs[:4]
        latest_refs, refs = refs[4 : 4 + len(latest)], refs[4 + len(latest) + len(settled) :]
        if more:
            (next_out, u0_out, u1_out, z_out), refs = refs[:4], refs[4:]
        if ends:
            (kept_out, sent_out), refs = refs[:2], refs[2:]
        if not more:
            next_out = refs.pop(0)
        _, half, _ = place()

        def finish(which, slot, row, first, total):
            at = (slot, row, cut(first), slice(None))
            if split:
                last = merged(sizes, *latest_refs, slot, row, first)
            else:
                last = latest_refs[0][at]
            value = 2.0 * later_ref[at] - last + total
            next_out[at] = value
            if more:
                here = v_ref[at]
                value = here * here * value
                (u0_out, u1_out)[slot][row, cut(first), :] = value
                if which == slot:
                    z_out[flat(sizes, row, first)] = value

        sweep(sizes, partial_ref, beside_ref, finish)
        if ends:
            kept_out[...] = next_out[half, :, sizes.own(half), :]
            for row in range(sizes.rows):
                sent_out[pl.ds(row * sizes.half, sizes.half), :] = next_out[
                    1 - half, row, sizes.own(half), :
                ]
            rest = sent_out.shape[0] - sizes.rows * sizes.half
            sent_out[pl.ds(sizes.rows * sizes.half, rest), :] = jnp.zeros((rest, sizes.depth), F32)

    outs = []
    if more:
        outs += [(sizes.pair, VMEM)] + [(sizes.block, VMEM)] * 2 + [(sizes.edge, VMEM)]
    if ends:
        outs += [(sizes.sent, VMEM), (sizes.moved if more else sizes.back, VMEM)]
    return run(
        body,
        f"adjoint_{step_no}",
        (partial, beside, later, speed, *latest, *settled),
        [VMEM] * (4 + len(latest)) + [ANY] * len(settled),
        outs,
        [] if more else [sizes.pair],
    )


def forward_begin(sizes, own, moved, settled):
    def body(own_ref, moved_ref, *rest):
        c0_out, c1_out, z_out = rest[len(settled) :]
        _, _, core = place()

        def columns(first):
            for row in range(sizes.rows):
                pair = [merged(sizes, own_ref, moved_ref, slot, row, first) for slot in range(2)]
                c0_out[row, cut(first), :] = pair[0]
                c1_out[row, cut(first), :] = pair[1]
                z_out[flat(sizes, row, first)] = jnp.where(core == 0, *pair)

        over_columns(sizes.wide, columns)

    return run(
        body,
        "forward_begin",
        (own, moved, *settled),
        [VMEM] * 2 + [ANY] * len(settled),
        [(sizes.block, VMEM)] * 2 + [(sizes.edge, VMEM)],
    )


def forward_step(
    sizes, step_no, partial, current, before, speed, later, gradient, source, settled=()
):
    first_step = step_no == 1
    last_step = step_no == STEPS - 1

    def body(*refs):
        refs = list(refs)
        partial_ref, c_refs, beside_ref, v_ref, refs = refs[0], refs[1:3], refs[3], refs[4], refs[5:]
        late, refs = refs[: len(later)], refs[len(later) :]
        if not first_step:
            g_ref, refs = refs[0], refs[1:]
        before_refs, refs = refs[:2], refs[2:]
        (cells_ref, wavelet_ref, start_ref), refs = refs[:3], refs[3:]
        c0_out, c1_out, g_out, *z_outs = refs[len(settled) :]
        level, half, core = place()

        def finish(which, slot, row, first, total):
            at = (slot, row, cut(first), slice(None))
            if first_step:
                g_out[at] = total
            elif step_no == 2:
                g_out[at] = late[0][at] * g_ref[at] + late[1][at] * total
            else:
                g_out[at] = g_ref[at] + late[0][at] * total
            if first_step:
                last = merged(sizes, *before_refs, slot, row, first)
            else:
                last = before_refs[slot][row, cut(first), :]
            here = v_ref[at]
            centre = c_refs[slot][row, cut(first), :]
            value = 2.0 * centre - last + here * here * total
            (c0_out, c1_out)[slot][row, cut(first), :] = value
            if which == slot and not last_step:
                z_outs[0][flat(sizes, row, first)] = value

        sweep(sizes, partial_ref, beside_ref, finish)
        col = cells_ref[0, 1] - half * (sizes.half - EXTRA)
        pulse = wavelet_ref[0, start_ref[0] + step_no]
        for slot, c_out in enumerate((c0_out, c1_out)):
            row = cells_ref[0, 0] - ((level * 2 + slot) * 2 + core) * sizes.rows
            inside = (row >= 0) & (row < sizes.rows) & (col >= 0) & (col < sizes.wide)

            def put(out, at):
                hit = iota((1, sizes.depth), 1) == cells_ref[0, 2]
                out[at] = out[at] + jnp.where(hit, pulse, 0.0)

            pl.when(inside)(functools.partial(put, c_out, (row, pl.ds(col, 1), slice(None))))
            if last_step:

                z_outs[slot][...] = c_out[:, sizes.own(half), :]

                @pl.when(core == slot)
                def _():
                    for part, z_out in enumerate(z_outs[2:]):
                        here = pl.ds(
                            pl.multiple_of(half * EXTRA + part * sizes.quarter, 16), sizes.quarter
                        )
                        for line in range(sizes.rows):
                            z_out[pl.ds(line * sizes.quarter, sizes.quarter), :] = c_out[
                                line, here, :
                            ]

            else:
                pl.when(inside & (core == slot))(
                    functools.partial(
                        put, z_outs[0], (pl.ds(col + row * sizes.wide, 1), slice(None))
                    )
                )

    operands = (partial, *current, speed, *later)
    if not first_step:
        operands += (gradient,)
    operands += before
    specs = [VMEM] * len(operands) + [SMEM] * 3 + [ANY] * len(settled)
    outs = [(sizes.block, VMEM)] * 2 + [(sizes.pair, VMEM)]
    if last_step:
        outs += [(sizes.sent, VMEM)] * 2 + [(sizes.edges, VMEM)] * 2
    else:
        outs += [(sizes.edge, VMEM)]
    return run(body, f"forward_{step_no}", (*operands, *source, *settled), specs, outs)


def forward_end(sizes, part, partial, beside, speed, later, gradient, settled=()):
    def body(partial_ref, beside_ref, v_ref, later_ref, g_ref, *rest):
        kept_out, sent_out, both = rest[len(settled) :]
        _, half, core = place()
        rows = sizes.rows
        for which in range(2):

            @pl.when(core == which)
            def _():
                @pl.loop(0, sizes.quarter // 8)
                def _(step):
                    local = pl.multiple_of(step * 8, 8)
                    first = pl.multiple_of(half * EXTRA + part * sizes.quarter + local, 8)
                    far = [
                        beside_ref[pl.ds(pl.multiple_of(local + row * sizes.quarter, 8), 8), :]
                        for row in range(rows)
                    ]
                    for slot in range(2):
                        for row in range(rows):
                            at = (slot, row, cut(first), slice(None))
                            total = partial_ref[at]
                            for offset in range(1, REACH + 1):
                                line = row + offset - rows if which else row - offset + rows
                                if slot == which and 0 <= line < rows:
                                    total = total + WEIGHTS[offset] * far[line]
                            total = g_ref[at] + later_ref[at] * total
                            both[slot, row, cut(local), :] = 2.0 * v_ref[at] * total

        kept_out[...] = both[half]
        sent_out[...] = both[1 - half]

    return run(
        body,
        f"forward_end_{part}",
        (partial, beside, speed, later, gradient, *settled),
        [VMEM] * 5 + [ANY] * len(settled),
        [(sizes.quarters, VMEM)] * 2,
        [(2, *sizes.quarters)],
    )


def fill_gradient(sizes, parts, whole=None):
    arrays = [array for _, _, array in parts]
    given = () if whole is None else (whole,)

    def body(*refs):
        out, sems = refs[-2], refs[-1]
        _, half, _ = place()
        copies = Copies(sems)
        for (part, received, _), ref in zip(parts, refs):
            side = 1 - half if received else half
            first = pl.multiple_of(side * sizes.half + part * sizes.quarter, 16)
            copies.start(ref, out.at[:, pl.ds(first, sizes.quarter), :])
        copies.wait()

    return run(
        body,
        f"fill_gradient_{len(given)}",
        (*arrays, *given),
        [ANY] * (len(arrays) + len(given)),
        [(sizes.whole, ANY)],
        aliases={len(arrays): 0} if given else None,
        sems=len(parts),
    )[0]


def fill(sizes, shape, parts, name):
    def body(*refs):
        out, sems = refs[-2], refs[-1]
        _, half, _ = place()
        copies = Copies(sems)
        for index, ref in enumerate(refs[:-2]):
            target = out.at[index // 2, 0] if len(shape) == 5 else out
            side = half if index % 2 == 0 else 1 - half
            if len(ref.shape) == 2:
                ref = ref.at[pl.ds(0, sizes.rows * sizes.half)].reshape(sizes.sent)
            copies.start(ref, target.at[:, sizes.final(side), :])
        copies.wait()

    return run(
        body, name, parts, [ANY] * len(parts), [(shape, ANY)], sems=len(parts)
    )[0]


def on_device(
    wave_state, adjoint_state, velocity, wavelet, traces, source_cells, receiver_cells, start_step
):
    count = lax.axis_size("gx")
    sizes = Sizes(*velocity.shape)
    across = [(i, i ^ 2) for i in range(count)]
    cores = [(i, i ^ 1) for i in range(count)]
    levels = []
    for level in range(count // 4 - 1):
        for half in range(2):
            low, high = 4 * level + 2 * half + 1, 4 * level + 4 + 2 * half
            levels += [(low, high), (high, low)]
    halves = [[i for i in range(count) if (i % 4) // 2 == half] for half in range(2)]

    def over(field):
        return lax.ppermute(field, "gx", across)

    def exchange(block0, block1, edge):
        return (
            block0,
            block1,
            lax.ppermute(block0, "gx", cores),
            lax.ppermute(block1, "gx", cores),
            lax.ppermute(edge, "gx", levels),
        )

    each, steps = traces.shape[2], traces.shape[1]
    sent = pack_first(sizes, velocity, traces[0].T) + pack(sizes, adjoint_state, wave_state)
    velocity_in, later_in, latest_in, current_in, before_in = map(over, sent)
    kept = keep(sizes, velocity, adjoint_state, wave_state)

    speed, tails = speed_begin(sizes, kept[0], velocity_in, sent[0])
    tails = lax.all_gather(tails, "gx", axis_index_groups=halves)
    tails = tails[:, :, :each, :steps].reshape(count // 4, 2, 2, each, steps)
    samples = tails.transpose(4, 0, 2, 1, 3).reshape(1, steps, count * each)
    samples = lax.dynamic_slice_in_dim(samples, start_step[0] + 1, STEPS, 1)

    adjoint = functools.partial(adjoint_step, sizes)
    forward = functools.partial(forward_step, sizes)
    source = (source_cells, wavelet, start_step)

    def ready(step_no, blocks, settled=()):
        return prepare(
            sizes,
            blocks[:4],
            f"prepare_adjoint_{step_no}",
            (step_no, receiver_cells, samples),
            settled,
        )

    def ready_forward(step_no, blocks, settled=()):
        partial = prepare(
            sizes, blocks[:4], f"prepare_forward_{step_no}", settled=settled
        )
        return partial, (*blocks[:2], blocks[4])

    later4, *scaled = adjoint_begin(sizes, speed, kept[1], later_in, samples)
    scaled = exchange(*scaled)
    later3, *scaled = adjoint(
        4, ready(4, scaled), scaled[4], later4, (kept[2], latest_in), speed
    )
    scaled = exchange(*scaled)
    current1 = exchange(*forward_begin(sizes, kept[3], current_in, scaled[:1]))
    later2, *scaled = adjoint(
        3, ready(3, scaled, scaled[4:]), scaled[4], later3, (later4,), speed, current1[:1]
    )
    scaled = exchange(*scaled)
    *current2, image, edge = forward(
        1, *ready_forward(1, current1, (before_in,)), (kept[4], before_in), speed, (), None, source
    )
    current2 = exchange(*current2, edge)
    later1, *scaled, mine1, sent1 = adjoint(
        2, ready(2, scaled), scaled[4], later2, (later3,), speed, current2[:1]
    )
    got1 = over(sent1)
    scaled = exchange(*scaled)
    partial = ready(1, scaled)
    *current3, gradient, edge = forward(
        2,
        *ready_forward(2, current2),
        current1[:2],
        speed,
        (later1, later2),
        image,
        source,
        scaled[2:4],
    )
    current3 = exchange(*current3, edge)
    prepared = ready_forward(3, current3)
    mine0, sent0 = adjoint(1, partial, scaled[4], later1, (later2,), speed, current3[2:4])
    got0 = over(sent0)
    *current4, gradient, narrow0, narrow1, edge0, edge1 = forward(
        3, *prepared, current2[:2], speed, (later3,), gradient, source, (mine0, got1)
    )
    *narrow4, beside0 = exchange(narrow0, narrow1, edge0)[2:]
    beside1 = lax.ppermute(edge1, "gx", levels)
    partial = prepare(sizes, (*current4, *narrow4), "prepare_forward_4", narrow=True)
    ends = functools.partial(forward_end, sizes)
    kept0, sent = ends(0, partial, beside0, speed, later4, gradient)
    moved0 = over(sent)
    kept1, sent = ends(1, partial, beside1, speed, later4, gradient, (kept0, got0))
    moved1 = over(sent)
    total = fill_gradient(sizes, [(0, False, kept0), (1, False, kept1), (0, True, moved0)])
    return fill_gradient(sizes, [(1, True, moved1)], total), fill(
        sizes, adjoint_state.shape, [mine0, got0, mine1, got1], "fill_adjoint"
    )


def solution(mesh):
    in_specs = (
        P(None, "groups", "gx", None, None),
        P(None, "groups", "gx", None, None),
        P("gx", "groups", None),
        P("groups", None),
        P("groups", None, "gx"),
        P("groups", None),
        P("groups", None, None),
        P("groups"),
    )
    out_specs = (P("gx", "groups", None), P(None, "groups", "gx", None, None))
    return jax.shard_map(
        on_device, mesh=mesh, in_specs=in_specs, out_specs=out_specs, check_vma=False
    )
```

```python
import functools

import jax
import jax.numpy as jnp
from jax import lax
from jax.experimental import pallas as pl
from jax.experimental.pallas import tpu as pltpu
from jax.sharding import PartitionSpec as P

STEPS = 4
WEIGHTS = (-205.0 / 72.0, 8.0 / 5.0, -1.0 / 5.0, 8.0 / 315.0, -1.0 / 560.0)
UNIT = WEIGHTS[1]
REACH = 4
EXTRA = REACH * STEPS
F32 = jnp.float32
BF16 = jnp.bfloat16
ANY = pl.BlockSpec(memory_space=pl.ANY)
VMEM = pl.BlockSpec(memory_space=pltpu.VMEM)
SMEM = pl.BlockSpec(memory_space=pltpu.SMEM)
MIB = 2**20
PACK_LIMIT = 56


def place():
    position = lax.axis_index("gx")
    return position // 4, (position % 4) // 2, position % 2


def banded(apart):
    band = jnp.zeros(apart.shape, F32)
    for offset in range(1, REACH + 1):
        band = jnp.where(jnp.abs(apart) == offset, WEIGHTS[offset] / UNIT, band)
    return band.astype(BF16)


def iota(shape, axis):
    return lax.broadcasted_iota(jnp.int32, shape, axis)


def two_terms(value):
    high = value.astype(BF16)
    return high, (value - high.astype(F32)).astype(BF16)


def dot(left, right, contract=((1,), (0,))):
    return lax.dot_general(left, right, (contract, ((), ())), preferred_element_type=F32)


class Copies:
    def __init__(self, sems):
        self.sems, self.going = sems, []

    def start(self, source, target):
        copy = pltpu.make_async_copy(source, target, self.sems.at[len(self.going)])
        copy.start()
        self.going.append(copy)

    def wait(self):
        for copy in self.going:
            copy.wait()


class Sizes:
    def __init__(self, rows, cols, depth):
        self.rows, self.cols, self.depth = rows, cols, depth
        self.half = cols // 2
        self.wide = self.half + EXTRA
        self.pair = (2, rows, self.wide, depth)
        self.block = (rows, self.wide, depth)
        self.edge = (rows * self.wide + 8, depth)
        self.moved = (rows * self.wide + 16, depth)
        self.sent = (rows, self.half, depth)
        self.whole = (rows, cols, depth)
        self.back = (rows * self.half + 8, depth)
        self.quarter = cols // 4
        self.quarters = (rows, self.quarter, depth)
        self.edges = (rows * self.quarter, depth)

    def window(self, half):
        return pl.ds(pl.multiple_of(half * (self.half - EXTRA), 16), self.wide)

    def own(self, half):
        return pl.ds(pl.multiple_of(half * EXTRA, 16), self.half)

    def final(self, half):
        return pl.ds(pl.multiple_of(half * self.half, 16), self.half)

    def moved_row(self, row):
        return pl.ds(row * self.wide, self.wide)

    @property
    def moved_tail(self):
        return pl.ds(self.rows * self.wide, 16)


def over_columns(count, body):
    @pl.loop(0, count // 16)
    def _(step):
        for part in range(2):
            body(pl.multiple_of(step * 16 + part * 8, 8))


def cut(first):
    return pl.ds(first, 8)


def flat(sizes, row, first):
    return pl.ds(pl.multiple_of(first + row * sizes.wide, 8), 8), slice(None)


def merged(sizes, own, moved, slot, row, first):
    _, half, _ = place()
    received = moved[flat(sizes, row, first)]
    return jnp.where(half == slot, own[row, cut(first), :], received)


def differences(sizes, blocks, mixed, added=None):
    wide, depth = sizes.wide, sizes.depth
    shape = (wide, 2 * wide)
    column = iota(shape, 1)
    column = jnp.where(column >= wide, column - wide, column)
    band_y = banded(iota(shape, 0) - column)
    shape = (2 * depth, depth)
    layer = iota(shape, 0)
    layer = jnp.where(layer >= depth, layer - depth, layer)
    band_z = banded(layer - iota(shape, 1))
    for slot in range(2):
        for row in range(sizes.rows):
            terms = two_terms(blocks[slot][row])
            total = dot(jnp.concatenate(terms, 1), band_z)
            total = UNIT * (total + dot(band_y, jnp.concatenate(terms, 0)))
            if added is not None:
                total = total + added(slot, row)
            mixed[slot, row] = total


def along_rows(sizes, blocks, mixed, partial, narrow=False):
    mine0, mine1, other0, other1 = blocks
    rows = sizes.rows
    _, half, core = place()
    orders = (
        (None, mine0, other0, mine1, other1),
        (other0, mine0, other1, mine1, None),
    )
    for which, order in enumerate(orders):

        @pl.when(core == which)
        def _():
            for slot in range(2):

                def columns(local):
                    first = local
                    if narrow:
                        first = pl.multiple_of(half * EXTRA + local, 8)
                    near = [
                        None
                        if block is None
                        else block[
                            row, cut(first if block is mine0 or block is mine1 else local), :
                        ]
                        for block in order[2 * slot : 2 * slot + 3]
                        for row in range(rows)
                    ]
                    for row in range(rows):
                        parts = []
                        for offset in range(1, REACH + 1):
                            pair = (near[rows + row + offset], near[rows + row - offset])
                            pair = [value for value in pair if value is not None]
                            if pair:
                                parts.append(WEIGHTS[offset] * sum(pair[1:], pair[0]))
                        total = 3.0 * WEIGHTS[0] * near[rows + row]
                        total = total + mixed[slot, row, cut(first), :]
                        partial[slot, row, cut(first), :] = sum(parts[1:], parts[0]) + total

                over_columns(sizes.half if narrow else sizes.wide, columns)


def prepare(sizes, blocks, name, inject=None, settled=(), narrow=False):
    def body(*refs):
        b_refs = refs[:4]
        partial, mixed = refs[-2:]
        added = None
        if inject is not None:
            step_no = inject[0]
            cells_ref, samples_ref = refs[4:6]
            level, half, core = place()
            where_x, where_y, where_z = (cells_ref[0, axis : axis + 1, :] for axis in range(3))
            count = where_x.shape[1]
            values = jnp.where(
                where_z == iota((sizes.depth, count), 0),
                samples_ref[0, step_no - 1 : step_no, :],
                0.0,
            )
            values = jnp.concatenate(two_terms(values), 1)
            col_ids = iota((sizes.wide, count), 0) + half * (sizes.half - EXTRA)

            def added(slot, row):
                this_row = ((level * 2 + slot) * 2 + core) * sizes.rows + row
                col_of = jnp.where(where_x == this_row, where_y, -1)
                hit = jnp.where(col_of == col_ids, 1.0, 0.0).astype(BF16)
                return dot(jnp.concatenate((hit, hit), 1), values, ((1,), (1,)))

        differences(sizes, b_refs, mixed, added)
        along_rows(sizes, b_refs, mixed, partial, narrow)

    operands = (*blocks, *(inject[1:] if inject is not None else ()))
    specs = [VMEM] * len(operands) + [ANY] * len(settled)
    return run(
        body,
        name,
        (*operands, *settled),
        specs,
        [(sizes.pair, VMEM)],
        [sizes.pair],
    )[0]


def sweep(sizes, partial, beside, finish):
    rows = sizes.rows
    _, _, core = place()
    for which in range(2):

        @pl.when(core == which)
        def _():
            def columns(first):
                far = [beside[flat(sizes, row, first)] for row in range(rows)]
                for slot in range(2):
                    for row in range(rows):
                        total = partial[slot, row, cut(first), :]
                        for offset in range(1, REACH + 1):
                            at = row + offset - rows if which else row - offset + rows
                            if slot == which and 0 <= at < rows:
                                total = total + WEIGHTS[offset] * far[at]
                        finish(which, slot, row, first, total)

            over_columns(sizes.wide, columns)


def run(body, name, operands, specs, outs, scratch=(), aliases=None, limit=24, sems=0):
    return pl.pallas_call(
        body,
        name=name,
        out_shape=[jax.ShapeDtypeStruct(shape, F32) for shape, _ in outs],
        in_specs=specs,
        out_specs=[spec for _, spec in outs],
        scratch_shapes=[pltpu.VMEM(shape, F32) for shape in scratch]
        + ([pltpu.SemaphoreType.DMA((sems,))] if sems else []),
        input_output_aliases=aliases or {},
        compiler_params=pltpu.CompilerParams(vmem_limit_bytes=limit * MIB),
        cost_estimate=pl.CostEstimate(flops=0, bytes_accessed=0, transcendentals=0),
    )(*operands)


def pack_first(sizes, velocity, traces):
    def body(field, traces_ref, out, sems):
        _, half, _ = place()
        copies = Copies(sems)
        copies.start(
            field.at[:, sizes.window(1 - half), :],
            out.at[pl.ds(0, sizes.rows * sizes.wide)].reshape(sizes.block),
        )
        each, steps = traces_ref.shape
        out[sizes.moved_tail, :] = jnp.zeros((16, sizes.depth), F32)
        out[pl.ds(sizes.rows * sizes.wide, each), :steps] = traces_ref[...]
        copies.wait()

    return run(
        body,
        "pack_first",
        (velocity, traces),
        [ANY, VMEM],
        [(sizes.moved, VMEM)],
        limit=16,
        sems=1,
    )


def pack(sizes, adjoint, wave):
    def body(a_ref, w_ref, *rest):
        outs, sems = rest[:4], rest[4]
        _, half, _ = place()
        copies = Copies(sems)
        fields = (a_ref.at[0, 0], a_ref.at[1, 0], w_ref.at[1, 0], w_ref.at[0, 0])
        for field, out in zip(fields, outs):
            copies.start(
                field.at[:, sizes.window(1 - half), :],
                out.at[pl.ds(0, sizes.rows * sizes.wide)].reshape(sizes.block),
            )
            tail = pl.ds(sizes.rows * sizes.wide, 8)
            out[tail, :] = jnp.zeros((8, sizes.depth), F32)
        copies.wait()

    return run(
        body,
        "pack",
        (adjoint, wave),
        [ANY] * 2,
        [(sizes.edge, VMEM)] * 4,
        limit=PACK_LIMIT,
        sems=4,
    )


def keep(sizes, velocity, adjoint, wave):
    def body(v_ref, a_ref, w_ref, *rest):
        outs, sems = rest[:5], rest[5]
        _, half, _ = place()
        copies = Copies(sems)
        fields = (v_ref, a_ref.at[0, 0], a_ref.at[1, 0], w_ref.at[1, 0], w_ref.at[0, 0])
        for field, out in zip(fields, outs):
            copies.start(field.at[:, sizes.window(half), :], out)
        copies.wait()

    return run(
        body,
        "keep",
        (velocity, adjoint, wave),
        [ANY] * 3,
        [(sizes.block, VMEM)] * 5,
        limit=PACK_LIMIT,
        sems=5,
    )


def speed_begin(sizes, own, moved, sent):
    def body(own_ref, moved_ref, sent_ref, v_out, tail_out):
        _, half, _ = place()
        tail_out[half] = sent_ref[sizes.moved_tail, :]
        tail_out[1 - half] = moved_ref[sizes.moved_tail, :]

        def columns(first):
            for slot in range(2):
                for row in range(sizes.rows):
                    v_out[slot, row, cut(first), :] = merged(
                        sizes, own_ref, moved_ref, slot, row, first
                    )

        over_columns(sizes.wide, columns)

    return run(
        body,
        "speed_begin",
        (own, moved, sent),
        [VMEM] * 3,
        [(sizes.pair, VMEM), ((2, 16, sizes.depth), VMEM)],
    )


def adjoint_begin(sizes, speed, own, moved, settled):
    def body(v_ref, own_ref, moved_ref, _, a_out, u0_out, u1_out, z_out):
        _, _, core = place()

        def columns(first):
            for slot, u_out in enumerate((u0_out, u1_out)):
                for row in range(sizes.rows):
                    value = merged(sizes, own_ref, moved_ref, slot, row, first)
                    a_out[slot, row, cut(first), :] = value
                    here = v_ref[slot, row, cut(first), :]
                    u_out[row, cut(first), :] = here * here * value
            for row in range(sizes.rows):
                z_out[flat(sizes, row, first)] = jnp.where(
                    core == 0, u0_out[row, cut(first), :], u1_out[row, cut(first), :]
                )

        over_columns(sizes.wide, columns)

    return run(
        body,
        "adjoint_begin",
        (speed, own, moved, settled),
        [VMEM] * 3 + [ANY],
        [(sizes.pair, VMEM)] + [(sizes.block, VMEM)] * 2 + [(sizes.edge, VMEM)],
    )


def adjoint_step(sizes, step_no, partial, beside, later, latest, speed, settled=()):
    split = len(latest) == 2
    more = step_no > 1
    ends = step_no <= 2

    def body(*refs):
        refs = list(refs)
        partial_ref, beside_ref, later_ref, v_ref = refs[:4]
        latest_refs, refs = refs[4 : 4 + len(latest)], refs[4 + len(latest) + len(settled) :]
        if more:
            (next_out, u0_out, u1_out, z_out), refs = refs[:4], refs[4:]
        if ends:
            (kept_out, sent_out), refs = refs[:2], refs[2:]
        if not more:
            next_out = refs.pop(0)
        _, half, _ = place()

        def finish(which, slot, row, first, total):
            at = (slot, row, cut(first), slice(None))
            if split:
                last = merged(sizes, *latest_refs, slot, row, first)
            else:
                last = latest_refs[0][at]
            value = 2.0 * later_ref[at] - last + total
            next_out[at] = value
            if more:
                here = v_ref[at]
                value = here * here * value
                (u0_out, u1_out)[slot][row, cut(first), :] = value
                if which == slot:
                    z_out[flat(sizes, row, first)] = value

        sweep(sizes, partial_ref, beside_ref, finish)
        if ends:
            kept_out[...] = next_out[half, :, sizes.own(half), :]
            for row in range(sizes.rows):
                sent_out[pl.ds(row * sizes.half, sizes.half), :] = next_out[
                    1 - half, row, sizes.own(half), :
                ]
            rest = sent_out.shape[0] - sizes.rows * sizes.half
            sent_out[pl.ds(sizes.rows * sizes.half, rest), :] = jnp.zeros((rest, sizes.depth), F32)

    outs = []
    if more:
        outs += [(sizes.pair, VMEM)] + [(sizes.block, VMEM)] * 2 + [(sizes.edge, VMEM)]
    if ends:
        outs += [(sizes.sent, VMEM), (sizes.moved if more else sizes.back, VMEM)]
    return run(
        body,
        f"adjoint_{step_no}",
        (partial, beside, later, speed, *latest, *settled),
        [VMEM] * (4 + len(latest)) + [ANY] * len(settled),
        outs,
        [] if more else [sizes.pair],
    )


def forward_begin(sizes, own, moved, settled):
    def body(own_ref, moved_ref, *rest):
        c0_out, c1_out, z_out = rest[len(settled) :]
        _, _, core = place()

        def columns(first):
            for row in range(sizes.rows):
                pair = [merged(sizes, own_ref, moved_ref, slot, row, first) for slot in range(2)]
                c0_out[row, cut(first), :] = pair[0]
                c1_out[row, cut(first), :] = pair[1]
                z_out[flat(sizes, row, first)] = jnp.where(core == 0, *pair)

        over_columns(sizes.wide, columns)

    return run(
        body,
        "forward_begin",
        (own, moved, *settled),
        [VMEM] * 2 + [ANY] * len(settled),
        [(sizes.block, VMEM)] * 2 + [(sizes.edge, VMEM)],
    )


def forward_step(
    sizes, step_no, partial, current, before, speed, later, gradient, source, settled=()
):
    first_step = step_no == 1
    last_step = step_no == STEPS - 1

    def body(*refs):
        refs = list(refs)
        partial_ref, c_refs, beside_ref, v_ref, refs = refs[0], refs[1:3], refs[3], refs[4], refs[5:]
        late, refs = refs[: len(later)], refs[len(later) :]
        if not first_step:
            g_ref, refs = refs[0], refs[1:]
        before_refs, refs = refs[:2], refs[2:]
        (cells_ref, wavelet_ref, start_ref), refs = refs[:3], refs[3:]
        c0_out, c1_out, g_out, *z_outs = refs[len(settled) :]
        level, half, core = place()

        def finish(which, slot, row, first, total):
            at = (slot, row, cut(first), slice(None))
            if first_step:
                g_out[at] = total
            elif step_no == 2:
                g_out[at] = late[0][at] * g_ref[at] + late[1][at] * total
            else:
                g_out[at] = g_ref[at] + late[0][at] * total
            if first_step:
                last = merged(sizes, *before_refs, slot, row, first)
            else:
                last = before_refs[slot][row, cut(first), :]
            here = v_ref[at]
            centre = c_refs[slot][row, cut(first), :]
            value = 2.0 * centre - last + here * here * total
            (c0_out, c1_out)[slot][row, cut(first), :] = value
            if which == slot and not last_step:
                z_outs[0][flat(sizes, row, first)] = value

        sweep(sizes, partial_ref, beside_ref, finish)
        col = cells_ref[0, 1] - half * (sizes.half - EXTRA)
        pulse = wavelet_ref[0, start_ref[0] + step_no]
        for slot, c_out in enumerate((c0_out, c1_out)):
            row = cells_ref[0, 0] - ((level * 2 + slot) * 2 + core) * sizes.rows
            inside = (row >= 0) & (row < sizes.rows) & (col >= 0) & (col < sizes.wide)

            def put(out, at):
                hit = iota((1, sizes.depth), 1) == cells_ref[0, 2]
                out[at] = out[at] + jnp.where(hit, pulse, 0.0)

            pl.when(inside)(functools.partial(put, c_out, (row, pl.ds(col, 1), slice(None))))
            if last_step:

                z_outs[slot][...] = c_out[:, sizes.own(half), :]

                @pl.when(core == slot)
                def _():
                    for part, z_out in enumerate(z_outs[2:]):
                        here = pl.ds(
                            pl.multiple_of(half * EXTRA + part * sizes.quarter, 16), sizes.quarter
                        )
                        for line in range(sizes.rows):
                            z_out[pl.ds(line * sizes.quarter, sizes.quarter), :] = c_out[
                                line, here, :
                            ]

            else:
                pl.when(inside & (core == slot))(
                    functools.partial(
                        put, z_outs[0], (pl.ds(col + row * sizes.wide, 1), slice(None))
                    )
                )

    operands = (partial, *current, speed, *later)
    if not first_step:
        operands += (gradient,)
    operands += before
    specs = [VMEM] * len(operands) + [SMEM] * 3 + [ANY] * len(settled)
    outs = [(sizes.block, VMEM)] * 2 + [(sizes.pair, VMEM)]
    if last_step:
        outs += [(sizes.sent, VMEM)] * 2 + [(sizes.edges, VMEM)] * 2
    else:
        outs += [(sizes.edge, VMEM)]
    return run(body, f"forward_{step_no}", (*operands, *source, *settled), specs, outs)


def forward_end(sizes, part, partial, beside, speed, later, gradient, settled=()):
    def body(partial_ref, beside_ref, v_ref, later_ref, g_ref, *rest):
        kept_out, sent_out, both = rest[len(settled) :]
        _, half, core = place()
        rows = sizes.rows
        for which in range(2):

            @pl.when(core == which)
            def _():
                @pl.loop(0, sizes.quarter // 8)
                def _(step):
                    local = pl.multiple_of(step * 8, 8)
                    first = pl.multiple_of(half * EXTRA + part * sizes.quarter + local, 8)
                    far = [
                        beside_ref[pl.ds(pl.multiple_of(local + row * sizes.quarter, 8), 8), :]
                        for row in range(rows)
                    ]
                    for slot in range(2):
                        for row in range(rows):
                            at = (slot, row, cut(first), slice(None))
                            total = partial_ref[at]
                            for offset in range(1, REACH + 1):
                                line = row + offset - rows if which else row - offset + rows
                                if slot == which and 0 <= line < rows:
                                    total = total + WEIGHTS[offset] * far[line]
                            total = g_ref[at] + later_ref[at] * total
                            both[slot, row, cut(local), :] = 2.0 * v_ref[at] * total

        kept_out[...] = both[half]
        sent_out[...] = both[1 - half]

    return run(
        body,
        f"forward_end_{part}",
        (partial, beside, speed, later, gradient, *settled),
        [VMEM] * 5 + [ANY] * len(settled),
        [(sizes.quarters, VMEM)] * 2,
        [(2, *sizes.quarters)],
    )


def fill_gradient(sizes, parts, whole=None):
    arrays = [array for _, _, array in parts]
    given = () if whole is None else (whole,)

    def body(*refs):
        out, sems = refs[-2], refs[-1]
        _, half, _ = place()
        copies = Copies(sems)
        for (part, received, _), ref in zip(parts, refs):
            side = 1 - half if received else half
            first = pl.multiple_of(side * sizes.half + part * sizes.quarter, 16)
            copies.start(ref, out.at[:, pl.ds(first, sizes.quarter), :])
        copies.wait()

    return run(
        body,
        f"fill_gradient_{len(given)}",
        (*arrays, *given),
        [ANY] * (len(arrays) + len(given)),
        [(sizes.whole, ANY)],
        aliases={len(arrays): 0} if given else None,
        sems=len(parts),
    )[0]


def fill(sizes, shape, parts, name):
    def body(*refs):
        out, sems = refs[-2], refs[-1]
        _, half, _ = place()
        copies = Copies(sems)
        for index, ref in enumerate(refs[:-2]):
            target = out.at[index // 2, 0] if len(shape) == 5 else out
            side = half if index % 2 == 0 else 1 - half
            if len(ref.shape) == 2:
                ref = ref.at[pl.ds(0, sizes.rows * sizes.half)].reshape(sizes.sent)
            copies.start(ref, target.at[:, sizes.final(side), :])
        copies.wait()

    return run(
        body, name, parts, [ANY] * len(parts), [(shape, ANY)], sems=len(parts)
    )[0]


def on_device(
    wave_state, adjoint_state, velocity, wavelet, traces, source_cells, receiver_cells, start_step
):
    count = lax.axis_size("gx")
    sizes = Sizes(*velocity.shape)
    across = [(i, i ^ 2) for i in range(count)]
    cores = [(i, i ^ 1) for i in range(count)]
    levels = []
    for level in range(count // 4 - 1):
        for half in range(2):
            low, high = 4 * level + 2 * half + 1, 4 * level + 4 + 2 * half
            levels += [(low, high), (high, low)]
    halves = [[i for i in range(count) if (i % 4) // 2 == half] for half in range(2)]

    def over(field):
        return lax.ppermute(field, "gx", across)

    def exchange(block0, block1, edge):
        return (
            block0,
            block1,
            lax.ppermute(block0, "gx", cores),
            lax.ppermute(block1, "gx", cores),
            lax.ppermute(edge, "gx", levels),
        )

    each, steps = traces.shape[2], traces.shape[1]
    sent = pack_first(sizes, velocity, traces[0].T) + pack(sizes, adjoint_state, wave_state)
    velocity_in, later_in, latest_in, current_in, before_in = map(over, sent)
    kept = keep(sizes, velocity, adjoint_state, wave_state)

    speed, tails = speed_begin(sizes, kept[0], velocity_in, sent[0])
    tails = lax.all_gather(tails, "gx", axis_index_groups=halves)
    tails = tails[:, :, :each, :steps].reshape(count // 4, 2, 2, each, steps)
    samples = tails.transpose(4, 0, 2, 1, 3).reshape(1, steps, count * each)
    samples = lax.dynamic_slice_in_dim(samples, start_step[0] + 1, STEPS, 1)

    adjoint = functools.partial(adjoint_step, sizes)
    forward = functools.partial(forward_step, sizes)
    source = (source_cells, wavelet, start_step)

    def ready(step_no, blocks, settled=()):
        return prepare(
            sizes,
            blocks[:4],
            f"prepare_adjoint_{step_no}",
            (step_no, receiver_cells, samples),
            settled,
        )

    def ready_forward(step_no, blocks, settled=()):
        partial = prepare(
            sizes, blocks[:4], f"prepare_forward_{step_no}", settled=settled
        )
        return partial, (*blocks[:2], blocks[4])

    later4, *scaled = adjoint_begin(sizes, speed, kept[1], later_in, samples)
    scaled = exchange(*scaled)
    later3, *scaled = adjoint(
        4, ready(4, scaled), scaled[4], later4, (kept[2], latest_in), speed
    )
    scaled = exchange(*scaled)
    current1 = exchange(*forward_begin(sizes, kept[3], current_in, scaled[:1]))
    later2, *scaled = adjoint(
        3, ready(3, scaled, scaled[4:]), scaled[4], later3, (later4,), speed, current1[:1]
    )
    scaled = exchange(*scaled)
    *current2, image, edge = forward(
        1, *ready_forward(1, current1, (before_in,)), (kept[4], before_in), speed, (), None, source
    )
    current2 = exchange(*current2, edge)
    later1, *scaled, mine1, sent1 = adjoint(
        2, ready(2, scaled), scaled[4], later2, (later3,), speed, current2[:1]
    )
    got1 = over(sent1)
    scaled = exchange(*scaled)
    partial = ready(1, scaled)
    *current3, gradient, edge = forward(
        2,
        *ready_forward(2, current2),
        current1[:2],
        speed,
        (later1, later2),
        image,
        source,
        scaled[2:4],
    )
    current3 = exchange(*current3, edge)
    prepared = ready_forward(3, current3)
    mine0, sent0 = adjoint(1, partial, scaled[4], later1, (later2,), speed, current3[:1])
    got0 = over(sent0)
    *current4, gradient, narrow0, narrow1, edge0, edge1 = forward(
        3, *prepared, current2[:2], speed, (later3,), gradient, source, (mine0, got1)
    )
    *narrow4, beside0 = exchange(narrow0, narrow1, edge0)[2:]
    beside1 = lax.ppermute(edge1, "gx", levels)
    partial = prepare(sizes, (*current4, *narrow4), "prepare_forward_4", narrow=True)
    ends = functools.partial(forward_end, sizes)
    kept0, sent = ends(0, partial, beside0, speed, later4, gradient)
    moved0 = over(sent)
    kept1, sent = ends(1, partial, beside1, speed, later4, gradient, (kept0, got0))
    moved1 = over(sent)
    total = fill_gradient(sizes, [(0, False, kept0), (1, False, kept1), (0, True, moved0)])
    return fill_gradient(sizes, [(1, True, moved1)], total), fill(
        sizes, adjoint_state.shape, [mine0, got0, mine1, got1], "fill_adjoint"
    )


def solution(mesh):
    in_specs = (
        P(None, "groups", "gx", None, None),
        P(None, "groups", "gx", None, None),
        P("gx", "groups", None),
        P("groups", None),
        P("groups", None, "gx"),
        P("groups", None),
        P("groups", None, None),
        P("groups"),
    )
    out_specs = (P("gx", "groups", None), P(None, "groups", "gx", None, None))
    return jax.shard_map(
        on_device, mesh=mesh, in_specs=in_specs, out_specs=out_specs, check_vma=False
    )
```
